128 devices in a mesh: seq: 32 (over y, z, x_lo), wt: 4 (over x_hi, core).
Axes of the slice: x: 4 (x_hi: 2, x_lo: 2; x = x_hi * 2 + x_lo), y: 4, z: 4, core: 2. Of those that a mesh axis runs over, the one named last changes fastest.
Arguments:
- tokens: float32 [4, 4096, 1024], P(None, 'seq'), may hold values from -6 to 6
- start_flags: int32 [4, 32], P(None, 'seq'), may hold values from 0 to 1, as said below
- norm_one: float32 [1024], replicated, may hold values from 0.5 to 1.5
- w_in: bfloat16 [3, 1024, 1024], P(None, None, 'wt'), may hold values from -0.1875 to 0.1875
- w_conv: float32 [3, 1024], P(None, 'wt'), may hold values from -3 to 3
- w_out: bfloat16 [1024, 1024], P(None, 'wt'), may hold values from -0.1875 to 0.1875
- norm_two: float32 [1024], replicated, may hold values from 0.5 to 1.5
- w_gate: bfloat16 [1024, 4608], P(None, 'wt'), may hold values from -0.1875 to 0.1875
- w_up: bfloat16 [1024, 4608], P(None, 'wt'), may hold values from -0.1875 to 0.1875
- w_down: bfloat16 [1024, 4608], P(None, 'wt'), may hold values from -0.1875 to 0.1875
- cotangent: float32 [4, 4096, 1024], P(None, 'seq'), may hold values from -6 to 6
Outputs:
- result: float32 [4, 4096, 1024], P(None, 'seq')
- grad_tokens: float32 [4, 4096, 1024], P(None, 'seq')
- grad_norm_one: float32 [1024], replicated
- grad_w_in: float32 [3, 1024, 1024], P(None, 'seq', 'wt')
- grad_w_conv: float32 [3, 1024], P(None, 'wt')
- grad_w_out: float32 [1024, 1024], P('seq', 'wt')
- grad_norm_two: float32 [1024], replicated
- grad_w_gate: float32 [1024, 4608], P('seq', 'wt')
- grad_w_up: float32 [1024, 4608], P('seq', 'wt')
- grad_w_down: float32 [1024, 4608], P('seq', 'wt')
The draws below stay inside these ranges and needn't reach their ends.
Inputs may be any that keep to these rules, and one draw needn't show every extreme that they name: start_flags[r, 0] is 1 for every row; in one row, drawn from the seed, no other entry is 1, so that row holds one sequence of all 4096 positions.
All inputs are finite; a program needn't handle non-finite values.
Results may differ from the reference program's by a relative error of at most 0.0093.
Values sent between devices are 32-bit elements; how exact they have to be, the bound alone decides.
A program may use at most 128 MiB of HBM per device.

```python
import jax
import jax.numpy as jnp
from jax import lax

D = 1024
FF = 4608
KERNEL = 3
ROWS = 4
TB = 128
L = 4096
N_SEQ = 32


def draw_start_flags(key, part):
    key = jax.random.fold_in(key, 11)
    key_row, key_bits = jax.random.split(key)
    whole_row = jax.random.randint(key_row, (), 0, ROWS)
    random_bits = (jax.random.randint(key_bits, (ROWS, N_SEQ), 0, 4) == 0).astype(jnp.int32)
    row_ids = lax.broadcasted_iota(jnp.int32, (ROWS, N_SEQ), 0)
    col_ids = lax.broadcasted_iota(jnp.int32, (ROWS, N_SEQ), 1)
    random_bits = jnp.where(row_ids == whole_row, 0, random_bits)
    return jnp.where(col_ids == 0, 1, random_bits).astype(jnp.int32)


def raised(values, rng, source, target, blocks, factor):
    owner, partner = [(jnp.arange(values.shape[axis_at]) // (values.shape[axis_at] // blocks)).reshape([-1 if axis == axis_at else 1 for axis in range(values.ndim)]) for axis_at in (source, target)]
    chosen = jax.random.permutation(rng, blocks)[partner]
    strong = (owner == chosen) | (owner == (partner + blocks // 2) % blocks)
    return jnp.where(strong, factor * values, values)


def levels(own_key, extent, shards, low, largest):
    def one(position, blocks):
        heights = jax.random.uniform(jax.random.fold_in(jax.random.fold_in(own_key, 6), position), (blocks,), jnp.float32, low / len(shards), largest / len(shards))
        return jnp.repeat(jnp.exp(heights), extent[position] // blocks).reshape((-1,) + (1,) * (len(extent) - position - 1))

    factor_of = one(*shards[0])
    for cut in shards[1:]:
        factor_of = factor_of * one(*cut)
    return factor_of


def centred(own_key, dims, deviation, most, shards=(), kind=jnp.bfloat16):
    gain = levels(own_key, dims, shards, -0.22, 0.18) if shards else 1.0
    values = jax.random.normal(own_key, dims, jnp.float32) * deviation * gain
    return jnp.minimum(jnp.maximum(values, -most), most).astype(kind)


def noise_with(rng, dims, spread, reach, shards, heavy, kind=jnp.bfloat16):
    array = spread * jax.random.normal(rng, dims, jnp.float32)
    if shards:
        array = array * levels(rng, dims, shards, -0.22, 0.18)
    return jnp.clip(raised(array, jax.random.fold_in(rng, 3), *heavy), -reach, reach).astype(kind)


def setup_inputs(seed: int = 0) -> dict:
    splits = jax.random.split(jax.random.key(seed), 12)
    tokens = noise_with(splits[0], (ROWS, L, D), 1.0, 6.0, ((1, 32),), (1, 2, 32, 2.75), jnp.float32)
    start_flags = draw_start_flags(jax.random.fold_in(splits[11], 71), 0)
    norm_one = jnp.clip(1.0 + 0.1 * jax.random.normal(splits[2], (D,), jnp.float32), 0.5, 1.5)
    w_in = centred(splits[3], (KERNEL, D, D), D ** -0.5, 0.1875, ((2, 4),))
    w_conv = centred(splits[4], (KERNEL, D), 0.6, 3.0, ((1, 4),), jnp.float32)
    w_out = centred(splits[5], (D, D), D ** -0.5, 0.1875, ((1, 4),))
    norm_two = jnp.clip(1.0 + 0.1 * jax.random.normal(splits[6], (D,), jnp.float32), 0.5, 1.5)
    w_gate = centred(splits[7], (D, FF), D ** -0.5, 0.1875, ((1, 4),))
    w_up = centred(splits[8], (D, FF), D ** -0.5, 0.1875, ((1, 4),))
    w_down = centred(splits[9], (D, FF), (FF // 4) ** -0.5, 0.1875, ((1, 4),))
    cotangent = noise_with(splits[10], (ROWS, L, D), 1.0, 6.0, ((1, 32),), (1, 2, 32, 2.75), jnp.float32)
    return {"tokens": tokens, "start_flags": start_flags, "norm_one": norm_one, "w_in": w_in, "w_conv": w_conv, "w_out": w_out, "norm_two": norm_two, "w_gate": w_gate, "w_up": w_up, "w_down": w_down, "cotangent": cotangent}


@jax.custom_vjp
def low(v):
    return lax.optimization_barrier(v.astype(jnp.bfloat16)).astype(jnp.float32)

@jax.custom_vjp
def low_back(v):
    return v

def low_keep(v):
    return (low(v), None)

def low_pass(kept, grad):
    return (grad,)

def back_keep(v):
    return (v, None)

def back_low(kept, grad):
    return (low(grad),)
low.defvjp(low_keep, low_pass)
low_back.defvjp(back_keep, back_low)
epsilon = 1e-05
highest = lax.Precision.HIGHEST

def rms_norm(values, gains):
    inverse = lax.rsqrt(lax.optimization_barrier(jnp.mean(values * values, axis=-1, keepdims=True)) + epsilon)
    return values * inverse * gains

def mixer_block(seq_row, starts, norm_one, w_in, w_conv, w_out, norm_two, w_gate, w_up, w_down):
    act_in = low(rms_norm(seq_row, norm_one))
    projected = low_back(jnp.einsum('td,jde->jte', act_in, w_in, precision=highest))
    gate_b, gate_c, value_x = (projected[0], projected[1], projected[2])
    product_bx = gate_b * value_x
    keep_one = 1.0 - starts
    keep_two = keep_one * jnp.concatenate([jnp.ones((1,), jnp.float32), keep_one[:-1]])
    width = product_bx.shape[1]
    back_one = jnp.concatenate([jnp.zeros((1, width), jnp.float32), product_bx[:-1]], axis=0)
    back_two = jnp.concatenate([jnp.zeros((2, width), jnp.float32), product_bx[:-2]], axis=0)
    conv_out = w_conv[0] * back_two * keep_two[:, None] + w_conv[1] * back_one * keep_one[:, None] + w_conv[2] * product_bx
    act_mix = low(gate_c * conv_out)
    branch = low_back(jnp.dot(act_mix, w_out.T, precision=highest))
    middle = seq_row + branch
    act_ffn = low(rms_norm(middle, norm_two))
    gate_pre = low_back(jnp.dot(act_ffn, w_gate, precision=highest))
    up_value = low_back(jnp.dot(act_ffn, w_up, precision=highest))
    hidden = low(jax.nn.silu(gate_pre) * up_value)
    ffn_out = low_back(jnp.dot(hidden, w_down.T, precision=highest))
    return middle + ffn_out

def reference(tokens, start_flags, norm_one, w_in, w_conv, w_out, norm_two, w_gate, w_up, w_down, cotangent):
    weights = (norm_one, w_in.astype(jnp.float32), w_conv, w_out.astype(jnp.float32), norm_two, w_gate.astype(jnp.float32), w_up.astype(jnp.float32), w_down.astype(jnp.float32))
    positions = jnp.arange(tokens.shape[1], dtype=jnp.int32)
    block_start = positions % TB == 0

    def one_row(totals, scanned):
        seq_row, row_flags, grad_out = scanned
        starts = jnp.where(block_start, row_flags[positions // TB], 0).astype(jnp.float32)

        def forward_row(values, *params):
            return mixer_block(values, starts, *params)
        output, pullback = jax.vjp(forward_row, seq_row, *weights)
        gradients = pullback(grad_out)
        totals = tuple((a + b for a, b in zip(totals, gradients[1:])))
        return (totals, (output, gradients[0]))
    zeros = tuple((jnp.zeros_like(w) for w in weights))
    totals, (result, grad_tokens) = lax.scan(one_row, zeros, (tokens, start_flags, cotangent))
    return (result, grad_tokens, totals[0], totals[1], totals[2], totals[3], totals[4], totals[5], totals[6], totals[7])
```

```python
import functools

import jax
import jax.numpy as jnp
from jax import lax
from jax.experimental import pallas as pl
from jax.experimental.pallas import tpu as pltpu
from jax.sharding import PartitionSpec as P

EPS = 1e-05
MESH = pl.DeviceIdType.MESH
F32 = jnp.float32
BF16 = jnp.bfloat16
NN = ((1,), (0,))
NT = ((1,), (1,))
TN = ((0,), (0,))

ROWS, TB, D, CH, HID = 4, 128, 1024, 256, 1152
POS = ROWS * TB
HALF = TB // 2
WIDTHS = (HID, HID, HID, 4 * CH)
TILES = ((0, 256), (256, 256), (512, 256), (768, 256), (1024, 128))


def mm(a, b, dims):
    return lax.dot_general(a, b, (dims, ((), ())), preferred_element_type=F32)


def kernel(
    flags, tokens, cotangent, w_in, w_out, w_gate, w_up, w_down, norm_one, norm_two, w_conv,
    result, grad_tokens, o_in, o_out, o_gate, o_up, o_down, o_small,
    tok, cot, win, wout, wg, wu, wd,
    act_in, proj, bxe, gce, conv, amix, mid, aff, hid, gg, gu, gf, gh, gbr, gproj, sbuf, hf, hb,
    part, c_recv, x_recv, a_recv,
    grads, rel1, fin1, rel2, fin2, last, small, ar,
    in_sem, out_sem, h_s, h_r, c_s, c_r, x_s, x_r, a_s, a_r,
    s1_s, s1_r, s2_s, s2_r, s3_s, s3_r, ar_s, ar_r, credit,
):
    s = lax.axis_index("seq")
    w = lax.axis_index("wt")
    y, z, l = s // 8, (s // 2) % 4, s % 2
    h, c = w // 2, w % 2

    def dev(y=y, z=z, l=l, h=h, c=c):
        return ((y * 4 + z) * 2 + l, h * 2 + c)

    def up(v, by=1):
        return (v + by) % 4

    plus = (dev(y=up(y)), dev(z=up(z)))
    minus = (dev(y=up(y, 3)), dev(z=up(z, 3)))
    across = dev(l=1 - l)
    far = dev(h=1 - h)
    mate = dev(c=1 - c)
    following = ((s + 1) % 32, w)
    previous = ((s + 31) % 32, w)

    def remote(src, dst, send, recv, to):
        copy = pltpu.make_async_remote_copy(
            src_ref=src, dst_ref=dst, send_sem=send, recv_sem=recv, device_id=to, device_id_type=MESH
        )
        copy.start()
        return copy

    loads = {}

    def load(name, src, dst):
        loads[name] = pltpu.make_async_copy(src, dst, in_sem.at[len(loads)])
        loads[name].start()

    load("tok", tokens, tok)
    load("win", w_in, win)
    load("wout", w_out, wout)
    load("cot", cotangent, cot)
    load("wd", w_down, wd)
    load("wg", w_gate, wg)
    load("wu", w_up, wu)

    barrier = pltpu.get_barrier_semaphore()
    partners = (
        plus + minus + (dev(y=up(y, 2)), dev(z=up(z, 2)), across, far, mate, following, previous)
    )
    for partner in partners:
        pl.semaphore_signal(barrier, inc=1, device_id=partner, device_id_type=MESH)

    small[...] = jnp.zeros_like(small)

    def rows_of(g):
        return pl.ds(g * 2 * TB, 2 * TB)

    keep = [1.0 - (flags[r, 0] == 1).astype(F32) for r in range(ROWS)]

    halo = {}

    def mixer_in(g):
        t = tok[2 * g : 2 * g + 2].reshape(2 * TB, D)
        scale = lax.rsqrt(jnp.mean(t * t, axis=-1, keepdims=True) + EPS)
        act = (t * scale * norm_one[...]).astype(BF16)
        act_in[rows_of(g)] = act
        for j in range(3):
            proj[j, rows_of(g)] = mm(act, win[j], NN)
        bx = proj[0, rows_of(g)] * proj[2, rows_of(g)]
        for k in range(2):
            bxe[2 * g + k, 8:] = bx[k * TB : (k + 1) * TB]

    def send_halo(g):
        for r in (2 * g, 2 * g + 1):
            halo[r] = remote(bxe.at[r, pl.ds(TB, 8)], hf.at[r], h_s.at[0, r], h_r.at[0, r], following)

    csend, xsend, asend = {}, {}, {}
    own = pl.ds(pl.multiple_of(c * HALF, HALF), HALF)
    other = pl.ds(pl.multiple_of((1 - c) * HALF, HALF), HALF)
    bank_of = (0, 1, 0, 1)

    def sum_begin(q, r):
        b = bank_of[q]
        csend[q, r] = remote(part.at[b, r, other], c_recv.at[b, r], c_s.at[q, r], c_r.at[q, r], mate)

    def sum_cross(q, r):
        b = bank_of[q]
        csend[q, r].wait_recv()
        part[b, r, own] = part[b, r, own] + c_recv[b, r]
        xsend[q, r] = remote(part.at[b, r, own], x_recv.at[(0, 1, 0, 2)[q], r], x_s.at[q, r], x_r.at[q, r], far)

    def sum_share(q, r):
        b = bank_of[q]
        xsend[q, r].wait()
        part[b, r, own] = part[b, r, own] + x_recv[(0, 1, 0, 2)[q], r]
        asend[q, r] = remote(part.at[b, r, own], a_recv.at[b, r], a_s.at[q, r], a_r.at[q, r], mate)

    def sum_end(q, r):
        b = bank_of[q]
        csend[q, r].wait_send()
        asend[q, r].wait()
        part[b, r, other] = a_recv[b, r]

    def mixer_out(g):
        for r in (2 * g, 2 * g + 1):
            rows = pl.ds(r * TB, TB)
            halo[r].wait()
            bxe[r, 0:8] = hf[r] * keep[r]
            total = (
                w_conv[0:1] * bxe[r, 6 : 6 + TB]
                + w_conv[1:2] * bxe[r, 7 : 7 + TB]
                + w_conv[2:3] * bxe[r, 8 : 8 + TB]
            )
            conv[rows] = total
            amix[rows] = (proj[1, rows] * total).astype(BF16)
        partial = mm(amix[rows_of(g)], wout[...], NT)
        for k in range(2):
            part[0, 2 * g + k] = partial[k * TB : (k + 1) * TB]
            sum_begin(0, 2 * g + k)

    def grad_hidden(g):
        value = cot[2 * g : 2 * g + 2].reshape(2 * TB, D).astype(BF16)
        gf[rows_of(g)] = value
        for n, width in TILES:
            gh[rows_of(g), n : n + width] = mm(value, wd[:, n : n + width], NN)

    def ffn(g):
        for r in (2 * g, 2 * g + 1):
            rows = pl.ds(r * TB, TB)
            m = tok[r] + part[0, r]
            mid[r] = m
            scale = lax.rsqrt(jnp.mean(m * m, axis=-1, keepdims=True) + EPS)
            aff[rows] = (m * scale * norm_two[...]).astype(BF16)
        act = aff[rows_of(g)]
        for n, width in TILES:
            at = (rows_of(g), pl.ds(n, width))
            gate = mm(act, wg[:, n : n + width], NN)
            upv = mm(act, wu[:, n : n + width], NN)
            sig = jax.nn.sigmoid(gate)
            silu = gate * sig
            grad = gh[at]
            hid[at] = (silu * upv).astype(BF16)
            gu[at] = (grad * silu).astype(BF16)
            gg[at] = (grad * upv * sig * (1.0 + gate * (1.0 - sig))).astype(BF16)

    def ffn_back(g):
        partial = mm(gg[rows_of(g)], wg[...], NT) + mm(gu[rows_of(g)], wu[...], NT)
        for k in range(2):
            part[1, 2 * g + k] = partial[k * TB : (k + 1) * TB]
            sum_begin(1, 2 * g + k)

    def ffn_out(g):
        partial = mm(hid[rows_of(g)], wd[...], NT)
        for k in range(2):
            part[1, 2 * g + k] = partial[k * TB : (k + 1) * TB]
            sum_begin(3, 2 * g + k)

    def product(slot, left, right, n, width):
        @pl.loop(0, 4)
        def _(i):
            columns = pl.ds(pl.multiple_of(i * 256, 256), 256)
            value = mm(left[:, columns], right, TN)
            grads[slot, i, :, :, :, n : n + width] = value.reshape(4, 2, 32, width)

    place = (y, z)

    def chunk(job, p, j, half=None):
        slot, width = job % 2, pl.ds(0, WIDTHS[job])
        cut = pl.ds(0, 4) if half is None else pl.ds(2 * half, 2)
        if p == 0:
            return grads.at[slot, j, cut, 0, :, width]
        return grads.at[slot, cut, j, 1, :, width]

    first = {}

    def ring_begin(job):
        slot, width = job % 2, pl.ds(0, WIDTHS[job])
        for p in range(2):
            i = place[p]
            if job >= 2:
                pl.semaphore_wait(credit.at[slot, p, 0], 1)
                pl.semaphore_wait(credit.at[slot, p, 1], 1)
            sems = lambda k: (s1_s.at[job, p, k], s1_r.at[job, p, k])
            first[job, p] = [
                remote(chunk(job, p, up(i, 2), 0), rel1.at[slot, p, 0, :, :, width], *sems(0), plus[p]),
                remote(chunk(job, p, up(i, 2), 1), rel1.at[slot, p, 1, :, :, width], *sems(1), minus[p]),
                remote(chunk(job, p, up(i), 1), fin1.at[slot, p, 0, pl.ds(2, 2), :, width], *sems(2), plus[p]),
                remote(chunk(job, p, up(i, 3), 0), fin1.at[slot, p, 1, pl.ds(0, 2), :, width], *sems(3), minus[p]),
            ]

    def ring_relay(job):
        slot, n = job % 2, WIDTHS[job]
        width = pl.ds(0, n)
        for p in range(2):
            i = place[p]
            copies = first[job, p]
            for k, j, half, to in ((0, up(i), 0, plus[p]), (1, up(i, 3), 1, minus[p])):
                copies[k].wait_recv()
                target = chunk(job, p, j, half)
                for m in range(2):
                    target[m] = target[m] + rel1[slot, p, k, m, :, :n]
                copies.append(
                    remote(
                        target, fin1.at[slot, p, k, pl.ds(2 * half, 2), :, width],
                        s1_s.at[job, p, 4 + k], s1_r.at[job, p, 4 + k], to,
                    )
                )

    second = {}

    def piece(job, p, j, half=None):
        slot, width = job % 2, pl.ds(0, WIDTHS[job])
        cut = pl.ds(0, 32) if half is None else pl.ds(16 * half, 16)
        if p == 0:
            return grads.at[slot, y, j, 0, cut, width]
        return grads.at[slot, j, z, 1, cut, width]

    def ring_turn(job):
        slot, n = job % 2, WIDTHS[job]
        width = pl.ds(0, n)
        for p in range(2):
            for k in (2, 3, 4, 5):
                first[job, p][k].wait_recv()
            mine = chunk(job, p, place[p])

            @pl.loop(0, 4)
            def _(m):
                mine[m] = mine[m] + fin1[slot, p, 0, m, :, :n] + fin1[slot, p, 1, m, :, :n]

            if job < 2:
                pl.semaphore_signal(credit.at[slot, p, 0], inc=1, device_id=minus[p], device_id_type=MESH)
                pl.semaphore_signal(credit.at[slot, p, 1], inc=1, device_id=plus[p], device_id_type=MESH)
            i = place[1 - p]
            sems = lambda k: (s2_s.at[job, p, k], s2_r.at[job, p, k])
            a, b = plus[1 - p], minus[1 - p]
            second[job, p] = [
                remote(piece(job, p, up(i, 2), 0), rel2.at[job, p, 0, :, width], *sems(0), a),
                remote(piece(job, p, up(i, 2), 1), rel2.at[job, p, 1, :, width], *sems(1), b),
                remote(piece(job, p, up(i), 1), fin2.at[job, p, 0, pl.ds(16, 16), width], *sems(2), a),
                remote(piece(job, p, up(i, 3), 0), fin2.at[job, p, 1, pl.ds(0, 16), width], *sems(3), b),
            ]

    def ring_relay_two(job):
        n = WIDTHS[job]
        width = pl.ds(0, n)
        for p in range(2):
            i = place[1 - p]
            copies = second[job, p]
            for k, j, half, to in ((0, up(i), 0, plus[1 - p]), (1, up(i, 3), 1, minus[1 - p])):
                copies[k].wait_recv()
                target = piece(job, p, j, half)
                target[...] = target[...] + rel2[job, p, k, :, :n]
                copies.append(
                    remote(
                        target, fin2.at[job, p, k, pl.ds(16 * half, 16), width],
                        s2_s.at[job, p, 4 + k], s2_r.at[job, p, 4 + k], to,
                    )
                )

    third = {}

    def ring_cross(job):
        slot, n = job % 2, WIDTHS[job]
        width = pl.ds(0, n)
        for p in range(2):
            for k in (2, 3, 4, 5):
                second[job, p][k].wait_recv()
            mine = piece(job, p, place[1 - p])
            mine[...] = mine[...] + fin2[job, p, 0, :, :n] + fin2[job, p, 1, :, :n]
        third[job] = remote(
            grads.at[slot, y, z, 1 - l, :, width], last.at[job, :, width], s3_s.at[job], s3_r.at[job], across
        )

    def ring_end(job):
        slot, n = job % 2, WIDTHS[job]
        third[job].wait()
        total = grads[slot, y, z, l, :, :n] + last[job, :, :n]
        if job < 3:
            (o_down, o_gate, o_up)[job][...] = total
        else:
            for j in range(3):
                o_in[j] = total[:, j * CH : (j + 1) * CH]
            o_out[...] = total[:, 3 * CH :]

    def ring_sent(job):
        for p in range(2):
            for copy in first[job, p] + second[job, p]:
                copy.wait_send()

    back = {}

    def mixer_back(g):
        for r in (2 * g, 2 * g + 1):
            rows = pl.ds(r * TB, TB)
            m, grad = mid[r], part[1, r]
            scale = lax.rsqrt(jnp.mean(m * m, axis=-1, keepdims=True) + EPS)
            small[0:1] += jnp.sum(grad * m * scale, axis=0, keepdims=True)
            weighted = grad * norm_two[...]
            total = (
                cot[r]
                + scale * weighted
                - m * (scale * scale * scale) * jnp.mean(weighted * m, axis=-1, keepdims=True)
            )
            cot[r] = total
            gbr[rows] = total.astype(BF16)
        gmix = mm(gbr[rows_of(g)], wout[...], NN)
        for k in range(2):
            r = 2 * g + k
            rows = pl.ds(r * TB, TB)
            value = gmix[k * TB : (k + 1) * TB]
            gproj[1, rows] = (value * conv[rows]).astype(BF16)
            gce[r, 0:TB] = value * proj[1, rows]
            sbuf[r] = gce[r, 0:8] * keep[r]
            back[r] = remote(sbuf.at[r], hb.at[r], h_s.at[1, r], h_r.at[1, r], previous)

    def mixer_back_in(g):
        for r in (2 * g, 2 * g + 1):
            rows = pl.ds(r * TB, TB)
            back[r].wait()
            gce[r, TB:] = hb[r]
            value = gce[r, 0:TB]
            for k in range(3):
                small[2 + k : 3 + k, 0:CH] += jnp.sum(
                    value * bxe[r, 6 + k : 6 + k + TB], axis=0, keepdims=True
                )
            gbx = w_conv[2:3] * value + w_conv[1:2] * gce[r, 1 : 1 + TB] + w_conv[0:1] * gce[r, 2 : 2 + TB]
            gproj[0, rows] = (gbx * proj[2, rows]).astype(BF16)
            gproj[2, rows] = (gbx * proj[0, rows]).astype(BF16)
        partial = mm(gproj[0, rows_of(g)], win[0], NT)
        for j in (1, 2):
            partial += mm(gproj[j, rows_of(g)], win[j], NT)
        for k in range(2):
            part[0, 2 * g + k] = partial[k * TB : (k + 1) * TB]
            sum_begin(2, 2 * g + k)

    outs = []

    def tokens_out(r):
        t, grad = tok[r], part[0, r]
        scale = lax.rsqrt(jnp.mean(t * t, axis=-1, keepdims=True) + EPS)
        small[1:2] += jnp.sum(grad * t * scale, axis=0, keepdims=True)
        weighted = grad * norm_one[...]
        cot[r] = (
            cot[r]
            + scale * weighted
            - t * (scale * scale * scale) * jnp.mean(weighted * t, axis=-1, keepdims=True)
        )
        outs.append(pltpu.make_async_copy(cot.at[r], grad_tokens.at[r], out_sem.at[r]))
        outs[-1].start()

    def result_out(r):
        mid[r] = mid[r] + part[1, r]
        outs.append(pltpu.make_async_copy(mid.at[r], result.at[r], out_sem.at[4 + r]))
        outs[-1].start()

    reduced = {}

    def small_begin(stage):
        at, peers = (
            (y, [dev(y=up(y, k)) for k in (1, 2, 3)]),
            (z, [dev(z=up(z, k)) for k in (1, 2, 3)]),
            (l, [across]),
        )[stage]
        ar[stage, at] = small[...]
        reduced[stage] = [
            remote(small, ar.at[stage, at], ar_s.at[stage, k], ar_r.at[stage, at], to)
            for k, to in enumerate(peers)
        ]

    def small_end(stage):
        at, count = ((y, 4), (z, 4), (l, 2))[stage]
        for k, copy in enumerate(reduced[stage]):
            copy.wait_send()
            there = (at + k + 1) % count
            pltpu.make_async_remote_copy(
                src_ref=small, dst_ref=ar.at[stage, there], send_sem=ar_s.at[stage, k],
                recv_sem=ar_r.at[stage, there], device_id=mate, device_id_type=MESH,
            ).wait_recv()
        total = ar[stage, 0] + ar[stage, 1]
        for k in range(2, count):
            total += ar[stage, k]
        small[...] = total

    loads["tok"].wait()
    loads["win"].wait()
    mixer_in(0)
    mixer_in(1)
    pl.semaphore_wait(barrier, len(partners))
    send_halo(0)
    send_halo(1)
    loads["wout"].wait()
    mixer_out(0)
    mixer_out(1)
    for r in range(4):
        sum_cross(0, r)
    loads["cot"].wait()
    loads["wd"].wait()
    grad_hidden(0)
    grad_hidden(1)
    loads["wg"].wait()
    loads["wu"].wait()
    sum_share(0, 0)
    sum_share(0, 1)
    sum_end(0, 0)
    sum_end(0, 1)
    ffn(0)
    ffn_back(0)
    sum_share(0, 2)
    sum_share(0, 3)
    sum_cross(1, 0)
    sum_cross(1, 1)
    sum_end(0, 2)
    sum_end(0, 3)
    ffn(1)
    product(0, gf, hid[...], 0, HID)
    ring_begin(0)
    ffn_back(1)
    sum_cross(1, 2)
    sum_cross(1, 3)
    product(1, aff, gg[...], 0, HID)
    ring_begin(1)
    sum_share(1, 0)
    sum_share(1, 1)
    sum_end(1, 0)
    sum_end(1, 1)
    mixer_back(0)
    mixer_back_in(0)
    sum_cross(2, 0)
    sum_cross(2, 1)
    ring_relay(0)
    sum_share(1, 2)
    sum_share(1, 3)
    sum_end(1, 2)
    sum_end(1, 3)
    mixer_back(1)
    mixer_back_in(1)
    sum_cross(2, 2)
    sum_cross(2, 3)
    ring_turn(0)
    ffn_out(0)
    ffn_out(1)
    ring_relay_two(0)
    ring_relay(1)
    for r in range(4):
        sum_cross(3, r)
    ring_cross(0)
    ring_end(0)
    ring_sent(0)
    product(0, aff, gu[...], 0, HID)
    ring_begin(2)
    for r in range(4):
        sum_share(2, r)
    for r in range(4):
        sum_end(2, r)
        tokens_out(r)
    small_begin(0)
    ring_turn(1)
    small_end(0)
    small_begin(1)
    ring_relay_two(1)
    small_end(1)
    small_begin(2)
    ring_cross(1)
    ring_end(1)
    small_end(2)
    ring_sent(1)
    for j in range(3):
        product(1, act_in, gproj[j], j * CH, CH)
    product(1, gbr, amix[...], 3 * CH, CH)
    ring_begin(3)
    o_small[...] = small[...]
    ring_relay(2)
    for r in range(4):
        sum_share(3, r)
    for r in range(4):
        sum_end(3, r)
        result_out(r)
    ring_turn(2)
    ring_relay_two(2)
    ring_relay(3)
    ring_cross(2)
    ring_turn(3)
    ring_end(2)
    ring_relay_two(3)
    ring_sent(2)
    ring_cross(3)
    ring_end(3)
    ring_sent(3)
    for copy in outs:
        copy.wait()


def on_device(
    tokens, start_flags, norm_one, w_in, w_conv, w_out, norm_two, w_gate, w_up, w_down, cotangent
):
    any_spec = pl.BlockSpec(memory_space=pl.ANY)
    vmem = pl.BlockSpec(memory_space=pltpu.VMEM)
    dma = pltpu.SemaphoreType.DMA
    shape = jax.ShapeDtypeStruct
    outs = pl.pallas_call(
        kernel,
        out_shape=(
            shape((ROWS, TB, D), F32),
            shape((ROWS, TB, D), F32),
            shape((3, 32, CH), F32),
            shape((32, CH), F32),
            shape((32, HID), F32),
            shape((32, HID), F32),
            shape((32, HID), F32),
            shape((8, D), F32),
        ),
        in_specs=[pl.BlockSpec(memory_space=pltpu.SMEM)] + [any_spec] * 7 + [vmem] * 3,
        out_specs=(any_spec, any_spec) + (vmem,) * 6,
        scratch_shapes=[
            pltpu.VMEM((ROWS, TB, D), F32),
            pltpu.VMEM((ROWS, TB, D), F32),
            pltpu.VMEM((3, D, CH), BF16),
            pltpu.VMEM((D, CH), BF16),
            pltpu.VMEM((D, HID), BF16),
            pltpu.VMEM((D, HID), BF16),
            pltpu.VMEM((D, HID), BF16),
            pltpu.VMEM((POS, D), BF16),
            pltpu.VMEM((3, POS, CH), F32),
            pltpu.VMEM((ROWS, TB + 8, CH), F32),
            pltpu.VMEM((ROWS, TB + 8, CH), F32),
            pltpu.VMEM((POS, CH), F32),
            pltpu.VMEM((POS, CH), BF16),
            pltpu.VMEM((ROWS, TB, D), F32),
            pltpu.VMEM((POS, D), BF16),
            pltpu.VMEM((POS, HID), BF16),
            pltpu.VMEM((POS, HID), BF16),
            pltpu.VMEM((POS, HID), BF16),
            pltpu.VMEM((POS, D), BF16),
            pltpu.VMEM((POS, HID), F32),
            pltpu.VMEM((POS, D), BF16),
            pltpu.VMEM((3, POS, CH), BF16),
            pltpu.VMEM((ROWS, 8, CH), F32),
            pltpu.VMEM((ROWS, 8, CH), F32),
            pltpu.VMEM((ROWS, 8, CH), F32),
            pltpu.VMEM((2, ROWS, TB, D), F32),
            pltpu.VMEM((2, ROWS, HALF, D), F32),
            pltpu.VMEM((3, ROWS, HALF, D), F32),
            pltpu.VMEM((2, ROWS, HALF, D), F32),
            pltpu.VMEM((2, 4, 4, 2, 32, HID), F32),
            pltpu.VMEM((2, 2, 2, 2, 32, HID), F32),
            pltpu.VMEM((2, 2, 2, 4, 32, HID), F32),
            pltpu.VMEM((4, 2, 2, 16, HID), F32),
            pltpu.VMEM((4, 2, 2, 32, HID), F32),
            pltpu.VMEM((4, 32, HID), F32),
            pltpu.VMEM((8, D), F32),
            pltpu.VMEM((3, 4, 8, D), F32),
            dma((7,)),
            dma((8,)),
            dma((2, 4)),
            dma((2, 4)),
            dma((4, 4)),
            dma((4, 4)),
            dma((4, 4)),
            dma((4, 4)),
            dma((4, 4)),
            dma((4, 4)),
            dma((4, 2, 6)),
            dma((4, 2, 6)),
            dma((4, 2, 6)),
            dma((4, 2, 6)),
            dma((4,)),
            dma((4,)),
            dma((3, 3)),
            dma((3, 4)),
            pltpu.SemaphoreType.REGULAR((2, 2, 2)),
        ],
        compiler_params=pltpu.CompilerParams(
            collective_id=0, has_side_effects=True, vmem_limit_bytes=63 * 2**20
        ),
        name="block",
    )(
        start_flags, tokens, cotangent, w_in, w_out, w_gate, w_up, w_down,
        norm_one.reshape(1, D), norm_two.reshape(1, D), w_conv,
    )
    result, grad_tokens, g_in, g_out, g_gate, g_up, g_down, g_small = outs
    return (
        result, grad_tokens, g_small[1], g_in, g_small[2:5, :CH], g_out, g_small[0], g_gate, g_up, g_down,
    )


def solution(mesh):
    return jax.shard_map(
        on_device,
        mesh=mesh,
        in_specs=(
            P(None, "seq", None),
            P(None, "seq"),
            P(),
            P(None, None, "wt"),
            P(None, "wt"),
            P(None, "wt"),
            P(),
            P(None, "wt"),
            P(None, "wt"),
            P(None, "wt"),
            P(None, "seq", None),
        ),
        out_specs=(
            P(None, "seq", None),
            P(None, "seq", None),
            P(),
            P(None, "seq", "wt"),
            P(None, "wt"),
            P("seq", "wt"),
            P(),
            P("seq", "wt"),
            P("seq", "wt"),
            P("seq", "wt"),
        ),
        check_vma=False,
    )
```

```python
import functools

import jax
import jax.numpy as jnp
from jax import lax
from jax.experimental import pallas as pl
from jax.experimental.pallas import tpu as pltpu
from jax.sharding import PartitionSpec as P

EPS = 1e-05
MESH = pl.DeviceIdType.MESH
F32 = jnp.float32
BF16 = jnp.bfloat16
NN = ((1,), (0,))
NT = ((1,), (1,))
TN = ((0,), (0,))

ROWS, TB, D, CH, HID = 4, 128, 1024, 256, 1152
POS = ROWS * TB
HALF = TB // 2
JOBS = (
    (0, 0, HID, 32),
    (1, 0, HID, 32),
    (0, 0, HID, 32),
    (1, 0, 3 * CH, 32),
    (1, 3 * CH, CH, 16),
)
TILES = ((0, 256), (256, 256), (512, 256), (768, 256), (1024, 128))


def mm(a, b, dims):
    return lax.dot_general(a, b, (dims, ((), ())), preferred_element_type=F32)


def kernel(
    flags, tokens, cotangent, w_in, w_out, w_gate, w_up, w_down, norm_one, norm_two, w_conv,
    result, grad_tokens, o_in, o_out, o_gate, o_up, o_down, o_small,
    tok, cot, win, wout, wg, wu, wd,
    proj, bxe, gce, mid, aff, hid, gg, gu, gf, gh, sbuf, hf, hb,
    part, c_recv, x_recv, a_recv,
    grads, rel1, fin1, rel2, fin2, last, grads_out, paired, small, ar,
    in_sem, out_sem, m_s, m_r, v_s, v_r, h_s, h_r, c_s, c_r, x_s, x_r, a_s, a_r,
    s1_s, s1_r, s2_s, s2_r, s3_s, s3_r, p_s, p_r, ar_s, ar_r, credit,
):
    s = lax.axis_index("seq")
    w = lax.axis_index("wt")
    y, z, l = s // 8, (s // 2) % 4, s % 2
    h, c = w // 2, w % 2

    def dev(y=y, z=z, l=l, h=h, c=c):
        return ((y * 4 + z) * 2 + l, h * 2 + c)

    def up(v, by=1):
        return (v + by) % 4

    plus = (dev(y=up(y)), dev(z=up(z)))
    minus = (dev(y=up(y, 3)), dev(z=up(z, 3)))
    across = dev(l=1 - l)
    far = dev(h=1 - h)
    mate = dev(c=1 - c)
    following = ((s + 1) % 32, w)
    previous = ((s + 31) % 32, w)

    def remote(src, dst, send, recv, to):
        copy = pltpu.make_async_remote_copy(
            src_ref=src, dst_ref=dst, send_sem=send, recv_sem=recv, device_id=to, device_id_type=MESH
        )
        copy.start()
        return copy

    loads = {}

    def load(name, src, dst):
        loads[name] = pltpu.make_async_copy(src, dst, in_sem.at[len(loads)])
        loads[name].start()

    load("wout", w_out, wout)
    load("tok", tokens, tok)
    load("win", w_in, win)
    load("cot", cotangent, cot)
    load("wd", w_down, wd)
    load("wg", w_gate, wg)
    load("wu", w_up, wu)

    barrier = pltpu.get_barrier_semaphore()
    partners = (
        plus + minus + (dev(y=up(y, 2)), dev(z=up(z, 2)), across, far, mate, following, previous)
    )
    for partner in partners:
        pl.semaphore_signal(barrier, inc=1, device_id=partner, device_id_type=MESH)

    small[...] = jnp.zeros_like(small)

    def rows_of(g):
        return pl.ds(g * 2 * TB, 2 * TB)

    keep = [1.0 - (flags[0, r] == 1).astype(F32) for r in range(ROWS)]

    halo = {}

    def normed(g):
        t = tok[2 * g : 2 * g + 2].reshape(2 * TB, D)
        scale = lax.rsqrt(jnp.mean(t * t, axis=-1, keepdims=True) + EPS)
        return (t * scale * norm_one[...]).astype(BF16)

    def mixer_in(g):
        act = normed(g)
        for j in range(3):
            proj[j, rows_of(g)] = mm(act, win[j], NN)
        bx = proj[0, rows_of(g)] * proj[2, rows_of(g)]
        for k in range(2):
            bxe[2 * g + k, 8:] = bx[k * TB : (k + 1) * TB]

    def send_halo(g):
        for r in (2 * g, 2 * g + 1):
            halo[r] = remote(bxe.at[r, pl.ds(TB, 8)], hf.at[r], h_s.at[0, r], h_r.at[0, r], following)

    mine = pl.ds(pl.multiple_of(w * CH, CH), CH)
    theirs = pl.ds(pl.multiple_of(((1 - h) * 2 + c) * CH, CH), CH)
    weight = {}

    def weight_begin():
        @pl.loop(0, 4)
        def _(i):
            rows = pl.ds(pl.multiple_of(i * 256, 256), 256)
            grads[1, i, :, :, :, mine] = wout[rows].astype(F32).reshape(4, 2, 32, CH)

    def weight_far():
        block = grads.at[1, y, z, :, :, mine]
        weight["far"] = remote(block, block, v_s.at[0], v_r.at[0], far)
        block = grads.at[1, :, :, :, :, mine]
        weight["mate"] = remote(block, block, v_s.at[1], v_r.at[1], mate)

    def weight_first():
        weight["far"].wait_recv()
        for p in range(2):
            for k in (1, 2, 3):
                to = dev(y=up(y, k)) if p == 0 else dev(z=up(z, k))
                block = grads.at[1, y, z, p, :, theirs]
                weight["first", p, k] = remote(
                    block, block, v_s.at[1 + p * 3 + k], v_r.at[1 + p * 3 + k], to
                )

    def weight_row(p, j):
        return grads.at[1, :, j, 0, :, theirs] if p == 0 else grads.at[1, j, :, 1, :, theirs]

    def weight_pass(p, k):
        block = weight_row(p, up((z, y)[p], 4 - k))
        weight["pass", p, k] = remote(
            block, block, v_s.at[14 + p * 4 + k], v_r.at[14 + p * 4 + k], mate
        )

    def weight_second():
        for p in range(2):
            for k in (1, 2, 3):
                weight["first", p, k].wait_recv()
        for p in range(2):
            for k in (1, 2, 3):
                to = dev(z=up(z, k)) if p == 0 else dev(y=up(y, k))
                block = weight_row(p, (z, y)[p])
                weight["second", p, k] = remote(
                    block, block, v_s.at[7 + p * 3 + k], v_r.at[7 + p * 3 + k], to
                )
        for p in range(2):
            weight_pass(p, 0)

    def weight_third():
        for k in (1, 3, 2):
            for p in range(2):
                weight["second", p, k].wait_recv()
                weight_pass(p, k)

    def weight_end():
        weight["mate"].wait()
        weight["far"].wait_send()
        for p in range(2):
            for k in (1, 2, 3):
                weight["first", p, k].wait_send()
                weight["second", p, k].wait_send()
            for k in range(4):
                weight["pass", p, k].wait()

    mix = {}

    def mix_block(k, columns):
        if k < 4:
            return part.at[0, k, pl.ds(8, TB - 8), columns]
        return part.at[0, :, pl.ds(0, 8), columns]

    def mix_send(k):
        block = mix_block(k, mine)
        mix["far", k] = remote(block, block, m_s.at[0, k], m_r.at[0, k], far)
        mix["mate", k] = remote(block, block, m_s.at[1, k], m_r.at[1, k], mate)

    def mix_pass(k):
        mix["far", k].wait_recv()
        block = mix_block(k, theirs)
        mix["pass", k] = remote(block, block, m_s.at[2, k], m_r.at[2, k], mate)

    def mix_end(k):
        mix["far", k].wait_send()
        mix["mate", k].wait()
        mix["pass", k].wait()

    def conv(r, at, count):
        return (
            w_conv[0:1] * bxe[r, at + 6 : at + 6 + count]
            + w_conv[1:2] * bxe[r, at + 7 : at + 7 + count]
            + w_conv[2:3] * bxe[r, at + 8 : at + 8 + count]
        )

    def taps(r, at, count):
        total = conv(r, at, count)
        rows = pl.ds(r * TB + at, count)
        part[0, r, at : at + count, mine] = (proj[1, rows] * total).astype(BF16).astype(F32)

    def mixer_out(g):
        for r in (2 * g, 2 * g + 1):
            taps(r, 8, TB - 8)
            mix_send(r)

    def mixer_edge():
        for r in range(4):
            halo[r].wait()
            bxe[r, 0:8] = hf[r] * keep[r]
            taps(r, 0, 8)
        mix_send(4)

    def branch(g):
        left = part[0, 2 * g : 2 * g + 2].reshape(2 * TB, D).astype(BF16)
        for i in range(4):
            right = grads[1, i, :, :, :, 0:D].reshape(256, D).astype(BF16)
            value = mm(left, right, NT).reshape(2, TB, 256)
            columns = pl.ds(i * 256, 256)
            mid[2 * g : 2 * g + 2, :, columns] = tok[2 * g : 2 * g + 2, :, columns] + value

    csend, xsend, asend = {}, {}, {}
    own = pl.ds(pl.multiple_of(c * HALF, HALF), HALF)
    other = pl.ds(pl.multiple_of((1 - c) * HALF, HALF), HALF)
    bank_of = (None, 1, 0, 1)

    def sum_begin(q, r):
        b = bank_of[q]
        csend[q, r] = remote(part.at[b, r, other], c_recv.at[b, r], c_s.at[q, r], c_r.at[q, r], mate)

    def sum_cross(q, r):
        b = bank_of[q]
        csend[q, r].wait_recv()
        part[b, r, own] = part[b, r, own] + c_recv[b, r]
        xsend[q, r] = remote(part.at[b, r, own], x_recv.at[q - 1, r], x_s.at[q, r], x_r.at[q, r], far)

    def sum_share(q, r):
        b = bank_of[q]
        xsend[q, r].wait()
        part[b, r, own] = part[b, r, own] + x_recv[q - 1, r]
        asend[q, r] = remote(part.at[b, r, own], a_recv.at[b, r], a_s.at[q, r], a_r.at[q, r], mate)

    def sum_end(q, r):
        b = bank_of[q]
        csend[q, r].wait_send()
        asend[q, r].wait()
        part[b, r, other] = a_recv[b, r]

    def grad_hidden(g):
        value = cot[2 * g : 2 * g + 2].reshape(2 * TB, D).astype(BF16)
        gf[rows_of(g)] = value
        for n, width in TILES:
            gh[rows_of(g), n : n + width] = mm(value, wd[:, n : n + width], NN)

    def ffn(g):
        for r in (2 * g, 2 * g + 1):
            rows = pl.ds(r * TB, TB)
            m = mid[r]
            scale = lax.rsqrt(jnp.mean(m * m, axis=-1, keepdims=True) + EPS)
            aff[rows] = (m * scale * norm_two[...]).astype(BF16)
        act = aff[rows_of(g)]
        for n, width in TILES:
            at = (rows_of(g), pl.ds(n, width))
            gate = mm(act, wg[:, n : n + width], NN)
            upv = mm(act, wu[:, n : n + width], NN)
            sig = jax.nn.sigmoid(gate)
            silu = gate * sig
            grad = gh[at]
            hid[at] = (silu * upv).astype(BF16)
            gu[at] = (grad * silu).astype(BF16)
            gg[at] = (grad * upv * sig * (1.0 + gate * (1.0 - sig))).astype(BF16)

    def ffn_back(g):
        partial = mm(gg[rows_of(g)], wg[...], NT) + mm(gu[rows_of(g)], wu[...], NT)
        for k in range(2):
            part[1, 2 * g + k] = partial[k * TB : (k + 1) * TB]
            sum_begin(1, 2 * g + k)

    def ffn_out(g):
        partial = mm(hid[rows_of(g)], wd[...], NT)
        for k in range(2):
            part[1, 2 * g + k] = partial[k * TB : (k + 1) * TB]
            sum_begin(3, 2 * g + k)

    def product(slot, left, right, n, width):
        @pl.loop(0, 4)
        def _(i):
            columns = pl.ds(pl.multiple_of(i * 256, 256), 256)
            value = mm(left[:, columns], right, TN)
            value = value.reshape(4, 2, 32, width)
            if slot is None:
                grads_out[i] = value
            else:
                grads[slot, i, :, :, :, n : n + width] = value

    place = (y, z)

    def block_of(job):
        slot, at, n, deep = JOBS[job]
        return slot, pl.ds(at, n), pl.ds(0, deep), deep

    def chunk(job, p, j, half=None):
        slot, columns, rows, deep = block_of(job)
        cut = pl.ds(0, 4) if half is None else pl.ds(2 * half, 2)
        if deep != 32:
            rows = pl.ds(deep * p, deep)
            return grads_out.at[j, cut, l, rows] if p == 0 else grads_out.at[cut, j, l, rows]
        if p == 0:
            return grads.at[slot, j, cut, 0, rows, columns]
        return grads.at[slot, cut, j, 1, rows, columns]

    pair = []

    def pair_begin():
        pair.append(remote(grads_out.at[:, :, 1 - l], paired, p_s.at[0], p_r.at[0], across))

    def pair_end():
        pair[0].wait()

        @pl.loop(0, 4)
        def _(i):
            grads_out[i, :, l] = grads_out[i, :, l] + paired[i]

    first = {}

    def ring_begin(job):
        slot, columns, rows, _ = block_of(job)
        for p in range(2):
            i = place[p]
            if job in (2, 3):
                pl.semaphore_wait(credit.at[slot, p, 0], 1)
                pl.semaphore_wait(credit.at[slot, p, 1], 1)
            sems = lambda k: (s1_s.at[job, p, k], s1_r.at[job, p, k])
            a, b = plus[p], minus[p]
            first[job, p] = [
                remote(chunk(job, p, up(i, 2), 0), rel1.at[slot, p, 0, :, rows, columns], *sems(0), a),
                remote(chunk(job, p, up(i, 2), 1), rel1.at[slot, p, 1, :, rows, columns], *sems(1), b),
                remote(chunk(job, p, up(i), 1), fin1.at[slot, p, 0, pl.ds(2, 2), rows, columns], *sems(2), a),
                remote(chunk(job, p, up(i, 3), 0), fin1.at[slot, p, 1, pl.ds(0, 2), rows, columns], *sems(3), b),
            ]

    def ring_relay(job):
        slot, columns, rows, _ = block_of(job)
        for p in range(2):
            i = place[p]
            copies = first[job, p]
            for k, j, half, to in ((0, up(i), 0, plus[p]), (1, up(i, 3), 1, minus[p])):
                copies[k].wait_recv()
                target = chunk(job, p, j, half)
                for m in range(2):
                    target[m] = target[m] + rel1[slot, p, k, m, rows, columns]
                copies.append(
                    remote(
                        target, fin1.at[slot, p, k, pl.ds(2 * half, 2), rows, columns],
                        s1_s.at[job, p, 4 + k], s1_r.at[job, p, 4 + k], to,
                    )
                )

    second = {}

    def piece(job, p, j, half=None):
        slot, columns, _, deep = block_of(job)
        row = (slot * 2 + p) * 128 + j * 32
        if half is None:
            return gh.at[pl.ds(pl.multiple_of(row, 32), deep), columns]
        return gh.at[pl.ds(pl.multiple_of(row + deep // 2 * half, 8), deep // 2), columns]

    def ring_turn(job):
        slot, columns, rows, deep = block_of(job)
        at, cut = min(job, 3), (pl.ds(0, deep // 2), pl.ds(deep // 2, deep // 2))
        for p in range(2):
            for k in (2, 3, 4, 5):
                first[job, p][k].wait_recv()
            mine = chunk(job, p, place[p])

            @pl.loop(0, 4)
            def _(m):
                to = pl.ds(pl.multiple_of((slot * 2 + p) * 128 + m * 32, 32), deep)
                gh[to, columns] = (
                    mine[m] + fin1[slot, p, 0, m, rows, columns] + fin1[slot, p, 1, m, rows, columns]
                )

            if job < 2:
                pl.semaphore_signal(credit.at[slot, p, 0], inc=1, device_id=minus[p], device_id_type=MESH)
                pl.semaphore_signal(credit.at[slot, p, 1], inc=1, device_id=plus[p], device_id_type=MESH)
            i = place[1 - p]
            sems = lambda k: (s2_s.at[job, p, k], s2_r.at[job, p, k])
            a, b = plus[1 - p], minus[1 - p]
            second[job, p] = [
                remote(piece(job, p, up(i, 2), 0), rel2.at[at, p, 0, cut[0], columns], *sems(0), a),
                remote(piece(job, p, up(i, 2), 1), rel2.at[at, p, 1, cut[0], columns], *sems(1), b),
                remote(piece(job, p, up(i), 1), fin2.at[at, p, 0, cut[1], columns], *sems(2), a),
                remote(piece(job, p, up(i, 3), 0), fin2.at[at, p, 1, cut[0], columns], *sems(3), b),
            ]

    def ring_relay_two(job):
        _, columns, _, deep = block_of(job)
        at, cut = min(job, 3), (pl.ds(0, deep // 2), pl.ds(deep // 2, deep // 2))
        for p in range(2):
            i = place[1 - p]
            copies = second[job, p]
            for k, j, half, to in ((0, up(i), 0, plus[1 - p]), (1, up(i, 3), 1, minus[1 - p])):
                copies[k].wait_recv()
                target = piece(job, p, j, half)
                target[...] = target[...] + rel2[at, p, k, cut[0], columns]
                copies.append(
                    remote(
                        target, fin2.at[at, p, k, cut[half], columns],
                        s2_s.at[job, p, 4 + k], s2_r.at[job, p, 4 + k], to,
                    )
                )

    third = {}

    def ring_cross(job):
        _, columns, rows, deep = block_of(job)
        at = min(job, 3)
        for p in range(2):
            for k in (2, 3, 4, 5):
                second[job, p][k].wait_recv()
            total = (
                piece(job, p, place[1 - p])[...]
                + fin2[at, p, 0, rows, columns]
                + fin2[at, p, 1, rows, columns]
            )
            if deep == 32:
                fin2[at, p, 0, :, columns] = total
            else:
                o_out[p * deep : (p + 1) * deep] = total
        if deep == 32:
            third[job] = remote(
                fin2.at[at, 1 - l, 0, :, columns], last.at[at, :, columns], s3_s.at[job], s3_r.at[job], across
            )

    def ring_end(job):
        columns = block_of(job)[1]
        third[job].wait()
        total = fin2[job, l, 0, :, columns] + last[job, :, columns]
        if job < 3:
            (o_down, o_gate, o_up)[job][...] = total
        else:
            for j in range(3):
                o_in[j] = total[:, j * CH : (j + 1) * CH]

    def ring_sent(job, copies):
        for p in range(2):
            for copy in copies[job, p]:
                copy.wait_send()

    back = {}

    def mixer_back(g):
        for r in (2 * g, 2 * g + 1):
            rows = pl.ds(r * TB, TB)
            m, grad = mid[r], part[1, r]
            scale = lax.rsqrt(jnp.mean(m * m, axis=-1, keepdims=True) + EPS)
            small[0:1] += jnp.sum(grad * m * scale, axis=0, keepdims=True)
            weighted = grad * norm_two[...]
            total = (
                cot[r]
                + scale * weighted
                - m * (scale * scale * scale) * jnp.mean(weighted * m, axis=-1, keepdims=True)
            )
            cot[r] = total
            gf[rows] = total.astype(BF16)
        gmix = mm(gf[rows_of(g)], wout[...], NN)
        for k in range(2):
            r = 2 * g + k
            rows = pl.ds(r * TB, TB)
            value = gmix[k * TB : (k + 1) * TB]
            total = conv(r, 0, TB)
            gg[rows, CH : 2 * CH] = (value * total).astype(BF16)
            wg[rows, 0:CH] = (proj[1, rows] * total).astype(BF16)
            gce[r, 0:TB] = value * proj[1, rows]
            sbuf[r] = gce[r, 0:8] * keep[r]
            back[r] = remote(sbuf.at[r], hb.at[r], h_s.at[1, r], h_r.at[1, r], previous)

    def mixer_back_in(g):
        for r in (2 * g, 2 * g + 1):
            rows = pl.ds(r * TB, TB)
            back[r].wait()
            gce[r, TB:] = hb[r]
            value = gce[r, 0:TB]
            for k in range(3):
                small[2 + k : 3 + k, 0:CH] += jnp.sum(
                    value * bxe[r, 6 + k : 6 + k + TB], axis=0, keepdims=True
                )
            gbx = w_conv[2:3] * value + w_conv[1:2] * gce[r, 1 : 1 + TB] + w_conv[0:1] * gce[r, 2 : 2 + TB]
            gg[rows, 0:CH] = (gbx * proj[2, rows]).astype(BF16)
            gg[rows, 2 * CH : 3 * CH] = (gbx * proj[0, rows]).astype(BF16)
        partial = mm(gg[rows_of(g), 0:CH], win[0], NT)
        for j in (1, 2):
            partial += mm(gg[rows_of(g), j * CH : (j + 1) * CH], win[j], NT)
        for k in range(2):
            part[0, 2 * g + k] = partial[k * TB : (k + 1) * TB]
            sum_begin(2, 2 * g + k)

    outs = []

    def tokens_out(r):
        t, grad = tok[r], part[0, r]
        scale = lax.rsqrt(jnp.mean(t * t, axis=-1, keepdims=True) + EPS)
        small[1:2] += jnp.sum(grad * t * scale, axis=0, keepdims=True)
        weighted = grad * norm_one[...]
        cot[r] = (
            cot[r]
            + scale * weighted
            - t * (scale * scale * scale) * jnp.mean(weighted * t, axis=-1, keepdims=True)
        )
        outs.append(pltpu.make_async_copy(cot.at[r], grad_tokens.at[r], out_sem.at[r]))
        outs[-1].start()

    def result_out(r):
        mid[r] = mid[r] + part[1, r]
        outs.append(pltpu.make_async_copy(mid.at[r], result.at[r], out_sem.at[4 + r]))
        outs[-1].start()

    reduced = {}

    def small_begin(stage):
        at, peers = (
            (y, [dev(y=up(y, k)) for k in (1, 2, 3)]),
            (z, [dev(z=up(z, k)) for k in (1, 2, 3)]),
            (l, [across]),
        )[stage]
        ar[stage, at] = small[...]
        reduced[stage] = [
            remote(small, ar.at[stage, at], ar_s.at[stage, k], ar_r.at[stage, at], to)
            for k, to in enumerate(peers)
        ]

    def small_end(stage):
        at, count = ((y, 4), (z, 4), (l, 2))[stage]
        for k, copy in enumerate(reduced[stage]):
            copy.wait_send()
            there = (at + k + 1) % count
            pltpu.make_async_remote_copy(
                src_ref=small, dst_ref=ar.at[stage, there], send_sem=ar_s.at[stage, k],
                recv_sem=ar_r.at[stage, there], device_id=mate, device_id_type=MESH,
            ).wait_recv()
        total = ar[stage, 0] + ar[stage, 1]
        for k in range(2, count):
            total += ar[stage, k]
        small[...] = total

    loads["wout"].wait()
    weight_begin()
    pl.semaphore_wait(barrier, len(partners))
    weight_far()
    loads["tok"].wait()
    loads["win"].wait()
    mixer_in(0)
    send_halo(0)
    mixer_out(0)
    mixer_in(1)
    send_halo(1)
    mixer_out(1)
    weight_first()
    loads["cot"].wait()
    loads["wd"].wait()
    grad_hidden(0)
    grad_hidden(1)
    weight_second()
    mixer_edge()
    mix_pass(0)
    mix_pass(1)
    mix_pass(2)
    weight_third()
    mix_pass(3)
    mix_pass(4)
    loads["wg"].wait()
    loads["wu"].wait()
    weight_end()
    mix_end(0)
    mix_end(1)
    mix_end(4)
    branch(0)
    ffn(0)
    mix_end(2)
    mix_end(3)
    branch(1)
    ffn(1)
    product(0, gf, hid[...], 0, HID)
    ring_begin(0)
    ffn_back(0)
    ffn_back(1)
    for r in range(4):
        sum_cross(1, r)
    product(1, aff, gg[...], 0, HID)
    ring_relay(0)
    ring_begin(1)
    sum_share(1, 0)
    sum_share(1, 1)
    sum_end(1, 0)
    sum_end(1, 1)
    mixer_back(0)
    ring_turn(0)
    ring_sent(0, first)
    product(0, aff, gu[...], 0, HID)
    ffn_out(0)
    sum_share(1, 2)
    sum_cross(3, 0)
    sum_cross(3, 1)
    ring_relay(1)
    ring_begin(2)
    sum_share(1, 3)
    sum_end(1, 2)
    sum_end(1, 3)
    mixer_back(1)
    product(None, gf, wg[0:POS, 0:CH], 0, CH)
    pair_begin()
    mixer_back_in(0)
    ffn_out(1)
    sum_cross(2, 0)
    sum_cross(2, 1)
    ring_relay_two(0)
    mixer_back_in(1)
    ring_turn(1)
    ring_sent(1, first)
    sum_cross(2, 2)
    sum_cross(2, 3)
    for g in (0, 1):
        aff[rows_of(g)] = normed(g)
    product(1, aff, gg[:, 0 : 3 * CH], 0, 3 * CH)
    ring_relay(2)
    ring_begin(3)
    pair_end()
    ring_begin(4)
    ring_cross(0)
    ring_relay_two(1)
    sum_share(3, 0)
    sum_share(3, 1)
    sum_cross(3, 2)
    sum_cross(3, 3)
    sum_share(2, 0)
    ring_sent(0, second)
    ring_relay(3)
    ring_relay(4)
    sum_share(2, 1)
    for r in (0, 1):
        sum_end(3, r)
        result_out(r)
        sum_end(2, r)
        tokens_out(r)
    ring_cross(1)
    ring_sent(1, second)
    ring_turn(2)
    sum_share(2, 2)
    ring_relay_two(2)
    ring_turn(3)
    ring_turn(4)
    sum_share(2, 3)
    for r in (2, 3):
        sum_end(2, r)
        tokens_out(r)
    small_begin(0)
    ring_cross(2)
    ring_relay_two(3)
    ring_relay_two(4)
    small_end(0)
    small_begin(1)
    ring_end(0)
    ring_end(1)
    ring_cross(3)
    ring_cross(4)
    small_end(1)
    small_begin(2)
    sum_share(3, 2)
    sum_share(3, 3)
    for r in (2, 3):
        sum_end(3, r)
        result_out(r)
    ring_end(2)
    small_end(2)
    o_small[...] = small[...]
    for job in range(5):
        if job >= 2:
            ring_sent(job, first)
            ring_sent(job, second)
    ring_end(3)
    for copy in outs:
        copy.wait()


def finish(*refs):
    ins, outs = refs[:8], refs[8:]
    outs[0][...] = ins[0][...]
    outs[1][...] = ins[1][...]

    @pl.when(pl.program_id(0) == 0)
    def _():
        for src, dst in zip(ins[2:7], outs[2:7]):
            dst[...] = src[...]
        small = ins[7]
        outs[7][...] = small[1]
        outs[8][...] = small[0]
        outs[9][...] = small[2:5, 0:CH]


def on_device(
    tokens, start_flags, norm_one, w_in, w_conv, w_out, norm_two, w_gate, w_up, w_down, cotangent
):
    any_spec = pl.BlockSpec(memory_space=pl.ANY)
    vmem = pl.BlockSpec(memory_space=pltpu.VMEM)
    dma = pltpu.SemaphoreType.DMA
    shape = jax.ShapeDtypeStruct
    outs = pl.pallas_call(
        kernel,
        out_shape=(
            shape((ROWS, TB, D), F32),
            shape((ROWS, TB, D), F32),
            shape((3, 32, CH), F32),
            shape((32, CH), F32),
            shape((32, HID), F32),
            shape((32, HID), F32),
            shape((32, HID), F32),
            shape((8, D), F32),
        ),
        in_specs=[pl.BlockSpec(memory_space=pltpu.SMEM)] + [any_spec] * 7 + [vmem] * 3,
        out_specs=(any_spec, any_spec) + (vmem,) * 6,
        scratch_shapes=[
            pltpu.VMEM((ROWS, TB, D), F32),
            pltpu.VMEM((ROWS, TB, D), F32),
            pltpu.VMEM((3, D, CH), BF16),
            pltpu.VMEM((D, CH), BF16),
            pltpu.VMEM((D, HID), BF16),
            pltpu.VMEM((D, HID), BF16),
            pltpu.VMEM((D, HID), BF16),
            pltpu.VMEM((3, POS, CH), F32),
            pltpu.VMEM((ROWS, TB + 8, CH), F32),
            pltpu.VMEM((ROWS, TB + 8, CH), F32),
            pltpu.VMEM((ROWS, TB, D), F32),
            pltpu.VMEM((POS, D), BF16),
            pltpu.VMEM((POS, HID), BF16),
            pltpu.VMEM((POS, HID), BF16),
            pltpu.VMEM((POS, HID), BF16),
            pltpu.VMEM((POS, D), BF16),
            pltpu.VMEM((POS, HID), F32),
                pltpu.VMEM((ROWS, 8, CH), F32),
            pltpu.VMEM((ROWS, 8, CH), F32),
            pltpu.VMEM((ROWS, 8, CH), F32),
            pltpu.VMEM((2, ROWS, TB, D), F32),
            pltpu.VMEM((2, ROWS, HALF, D), F32),
            pltpu.VMEM((3, ROWS, HALF, D), F32),
            pltpu.VMEM((2, ROWS, HALF, D), F32),
            pltpu.VMEM((2, 4, 4, 2, 32, HID), F32),
            pltpu.VMEM((2, 2, 2, 2, 32, HID), F32),
            pltpu.VMEM((2, 2, 2, 4, 32, HID), F32),
            pltpu.VMEM((4, 2, 2, 16, HID), F32),
            pltpu.VMEM((4, 2, 2, 32, HID), F32),
            pltpu.VMEM((4, 32, HID), F32),
            pltpu.VMEM((4, 4, 2, 32, CH), F32),
            pltpu.VMEM((4, 4, 32, CH), F32),
            pltpu.VMEM((8, D), F32),
            pltpu.VMEM((3, 4, 8, D), F32),
            dma((7,)),
            dma((8,)),
            dma((3, 5)),
            dma((3, 5)),
            dma((22,)),
            dma((22,)),
            dma((2, 4)),
            dma((2, 4)),
            dma((4, 4)),
            dma((4, 4)),
            dma((4, 4)),
            dma((4, 4)),
            dma((4, 4)),
            dma((4, 4)),
            dma((5, 2, 6)),
            dma((5, 2, 6)),
            dma((5, 2, 6)),
            dma((5, 2, 6)),
            dma((4,)),
            dma((4,)),
            dma((1,)),
            dma((1,)),
            dma((3, 3)),
            dma((3, 4)),
            pltpu.SemaphoreType.REGULAR((2, 2, 2)),
        ],
        compiler_params=pltpu.CompilerParams(
            collective_id=0, has_side_effects=True, vmem_limit_bytes=63 * 2**20
        ),
        name="block",
    )(
        start_flags.T, tokens, cotangent, w_in, w_out, w_gate, w_up, w_down,
        norm_one.reshape(1, D), norm_two.reshape(1, D), w_conv,
    )
    row = pl.BlockSpec((1, TB, D), lambda r: (r, 0, 0))

    def whole(array):
        return pl.BlockSpec(array.shape, lambda r: (0,) * array.ndim)

    result, grad_tokens, g_in, g_out, g_gate, g_up, g_down, one, two, taps = pl.pallas_call(
        finish,
        out_shape=tuple(shape(o.shape, F32) for o in outs[:2])
        + (
            shape((3, 32, CH), F32),
            shape((32, CH), F32),
            shape((32, HID), F32),
            shape((32, HID), F32),
            shape((32, HID), F32),
            shape((D,), F32),
            shape((D,), F32),
            shape((3, CH), F32),
        ),
        grid=(ROWS,),
        in_specs=[row, row] + [whole(o) for o in outs[2:]],
        out_specs=(row, row) + tuple(whole(o) for o in outs[2:7])
        + (pl.BlockSpec((D,), lambda r: (0,)),) * 2 + (pl.BlockSpec((3, CH), lambda r: (0, 0)),),
        name="finish",
    )(*outs)
    return result, grad_tokens, one, g_in, taps, g_out, two, g_gate, g_up, g_down


def solution(mesh):
    return jax.shard_map(
        on_device,
        mesh=mesh,
        in_specs=(
            P(None, "seq", None),
            P(None, "seq"),
            P(),
            P(None, None, "wt"),
            P(None, "wt"),
            P(None, "wt"),
            P(),
            P(None, "wt"),
            P(None, "wt"),
            P(None, "wt"),
            P(None, "seq", None),
        ),
        out_specs=(
            P(None, "seq", None),
            P(None, "seq", None),
            P(),
            P(None, "seq", "wt"),
            P(None, "wt"),
            P("seq", "wt"),
            P(),
            P("seq", "wt"),
            P("seq", "wt"),
            P("seq", "wt"),
        ),
        check_vma=False,
    )
```

```python
import functools

import jax
import jax.numpy as jnp
from jax import lax
from jax.experimental import pallas as pl
from jax.experimental.pallas import tpu as pltpu
from jax.sharding import PartitionSpec as P

EPS = 1e-05
MESH = pl.DeviceIdType.MESH
F32 = jnp.float32
BF16 = jnp.bfloat16
NN = ((1,), (0,))
NT = ((1,), (1,))
TN = ((0,), (0,))

ROWS, TB, D, CH, HID = 4, 128, 1024, 256, 1152
POS = ROWS * TB
HALF = TB // 2
JOBS = (
    (0, 0, HID, 32),
    (1, 0, HID, 32),
    (0, 0, HID, 32),
    (1, 0, 3 * CH, 32),
    (1, 3 * CH, CH, 16),
)
TILES = ((0, 256), (256, 256), (512, 256), (768, 256), (1024, 128))


def mm(a, b, dims):
    return lax.dot_general(a, b, (dims, ((), ())), preferred_element_type=F32)


def kernel(
    flags, tokens, cotangent, w_in, w_out, w_gate, w_up, w_down, norm_one, norm_two, w_conv,
    result, grad_tokens, o_in, o_out, o_gate, o_up, o_down, o_small,
    tok, cot, win, wout, wg, wu, wd,
    proj, bxe, gce, mid, aff, hid, gg, gu, gf, gh, sbuf, hf, hb,
    part, c_recv, x_recv, a_recv,
    grads, rel1, fin1, rel2, fin2, last, grads_out, paired, small, ar,
    in_sem, out_sem, m_s, m_r, v_s, v_r, h_s, h_r, c_s, c_r, x_s, x_r, a_s, a_r,
    s1_s, s1_r, split_s, split_r, s2_s, s2_r, s3_s, s3_r, p_s, p_r, ar_s, ar_r, credit,
):
    s = lax.axis_index("seq")
    w = lax.axis_index("wt")
    y, z, l = s // 8, (s // 2) % 4, s % 2
    h, c = w // 2, w % 2

    def dev(y=y, z=z, l=l, h=h, c=c):
        return ((y * 4 + z) * 2 + l, h * 2 + c)

    def up(v, by=1):
        return (v + by) % 4

    plus = (dev(y=up(y)), dev(z=up(z)))
    minus = (dev(y=up(y, 3)), dev(z=up(z, 3)))
    across = dev(l=1 - l)
    far = dev(h=1 - h)
    mate = dev(c=1 - c)
    following = ((s + 1) % 32, w)
    previous = ((s + 31) % 32, w)

    def remote(src, dst, send, recv, to):
        copy = pltpu.make_async_remote_copy(
            src_ref=src, dst_ref=dst, send_sem=send, recv_sem=recv, device_id=to, device_id_type=MESH
        )
        copy.start()
        return copy

    loads = {}

    def load(name, src, dst):
        loads[name] = pltpu.make_async_copy(src, dst, in_sem.at[len(loads)])
        loads[name].start()

    load("wout", w_out, wout)
    load("tok", tokens, tok)
    load("win", w_in, win)
    load("cot", cotangent, cot)
    load("wd", w_down, wd)
    load("wg", w_gate, wg)
    load("wu", w_up, wu)

    barrier = pltpu.get_barrier_semaphore()
    partners = (
        plus + minus + (dev(y=up(y, 2)), dev(z=up(z, 2)), across, far, mate, following, previous)
    )
    for partner in partners:
        pl.semaphore_signal(barrier, inc=1, device_id=partner, device_id_type=MESH)

    small[...] = jnp.zeros_like(small)

    def rows_of(g):
        return pl.ds(g * 2 * TB, 2 * TB)

    keep = [1.0 - (flags[0, r] == 1).astype(F32) for r in range(ROWS)]

    halo = {}

    def normed(g):
        t = tok[2 * g : 2 * g + 2].reshape(2 * TB, D)
        scale = lax.rsqrt(jnp.mean(t * t, axis=-1, keepdims=True) + EPS)
        return (t * scale * norm_one[...]).astype(BF16)

    def mixer_in(g):
        act = normed(g)
        for j in range(3):
            proj[j, rows_of(g)] = mm(act, win[j], NN)
        bx = proj[0, rows_of(g)] * proj[2, rows_of(g)]
        for k in range(2):
            bxe[2 * g + k, 8:] = bx[k * TB : (k + 1) * TB]

    def send_halo():
        halo[0] = remote(bxe.at[:, pl.ds(TB, 8)], hf, h_s.at[2], h_r.at[2], following)

    mine = pl.ds(pl.multiple_of(w * CH, CH), CH)
    theirs = pl.ds(pl.multiple_of(((1 - h) * 2 + c) * CH, CH), CH)
    weight = {}

    def weight_begin():
        @pl.loop(0, 4)
        def _(i):
            rows = pl.ds(pl.multiple_of(i * 256, 256), 256)
            grads[1, i, :, :, :, mine] = wout[rows].astype(F32).reshape(4, 2, 32, CH)

    def weight_far():
        block = grads.at[1, y, z, :, :, mine]
        weight["far"] = remote(block, block, v_s.at[0], v_r.at[0], far)
        block = grads.at[1, :, :, :, :, mine]
        weight["mate"] = remote(block, block, v_s.at[1], v_r.at[1], mate)

    def weight_first():
        weight["far"].wait_recv()
        for p in range(2):
            for k in (1, 2, 3):
                to = dev(y=up(y, k)) if p == 0 else dev(z=up(z, k))
                block = grads.at[1, y, z, p, :, theirs]
                weight["first", p, k] = remote(
                    block, block, v_s.at[1 + p * 3 + k], v_r.at[1 + p * 3 + k], to
                )

    def weight_row(p, j):
        return grads.at[1, :, j, 0, :, theirs] if p == 0 else grads.at[1, j, :, 1, :, theirs]

    def weight_pass(p, k):
        block = weight_row(p, up((z, y)[p], 4 - k))
        weight["pass", p, k] = remote(
            block, block, v_s.at[14 + p * 4 + k], v_r.at[14 + p * 4 + k], mate
        )

    def weight_second():
        for p in range(2):
            for k in (1, 2, 3):
                weight["first", p, k].wait_recv()
        for p in range(2):
            for k in (1, 2, 3):
                to = dev(z=up(z, k)) if p == 0 else dev(y=up(y, k))
                block = weight_row(p, (z, y)[p])
                weight["second", p, k] = remote(
                    block, block, v_s.at[7 + p * 3 + k], v_r.at[7 + p * 3 + k], to
                )
        for p in range(2):
            weight_pass(p, 0)

    def weight_third():
        for k in (1, 3, 2):
            for p in range(2):
                weight["second", p, k].wait_recv()
                weight_pass(p, k)

    def weight_near():
        weight["mate"].wait()

    def weight_end():
        weight["far"].wait_send()
        for p in range(2):
            for k in (1, 2, 3):
                weight["first", p, k].wait_send()
                weight["second", p, k].wait_send()
            for k in range(4):
                weight["pass", p, k].wait()

    mix = {}

    def mix_block(k, columns):
        if k < 2:
            return part.at[0, pl.ds(2 * k, 2), pl.ds(8, TB - 8), columns]
        return part.at[0, :, pl.ds(0, 8), columns]

    def mix_send(k):
        block = mix_block(k, mine)
        mix["far", k] = remote(block, block, m_s.at[0, k], m_r.at[0, k], far)
        mix["mate", k] = remote(block, block, m_s.at[1, k], m_r.at[1, k], mate)

    def mix_pass(k):
        mix["far", k].wait_recv()
        block = mix_block(k, theirs)
        mix["pass", k] = remote(block, block, m_s.at[2, k], m_r.at[2, k], mate)

    def mix_near(k):
        mix["mate", k].wait()

    def mix_end(k):
        mix["far", k].wait_send()
        mix["pass", k].wait()

    def conv(r, at, count):
        return (
            w_conv[0:1] * bxe[r, at + 6 : at + 6 + count]
            + w_conv[1:2] * bxe[r, at + 7 : at + 7 + count]
            + w_conv[2:3] * bxe[r, at + 8 : at + 8 + count]
        )

    def taps(r, at, count):
        total = conv(r, at, count)
        rows = pl.ds(r * TB + at, count)
        part[0, r, at : at + count, mine] = (proj[1, rows] * total).astype(BF16).astype(F32)

    def mixer_out(g):
        for r in (2 * g, 2 * g + 1):
            taps(r, 8, TB - 8)
        mix_send(g)

    def mixer_edge():
        halo[0].wait()
        for r in range(4):
            bxe[r, 0:8] = hf[r] * keep[r]
            taps(r, 0, 8)
        mix_send(2)

    def branch(chip, start):
        half = pl.ds(pl.multiple_of(chip * 2 * CH, 2 * CH), 2 * CH)
        left = part[0, :, :, half].reshape(POS, 2 * CH).astype(BF16)
        for i in range(4):
            right = grads[1, i, :, :, :, half].reshape(256, 2 * CH).astype(BF16)
            columns = pl.ds(i * 256, 256)
            mid[:, :, columns] = start[:, :, columns] + mm(left, right, NT).reshape(ROWS, TB, 256)

    csend, xsend, asend = {}, {}, {}
    own = pl.ds(pl.multiple_of(c * HALF, HALF), HALF)
    other = pl.ds(pl.multiple_of((1 - c) * HALF, HALF), HALF)
    bank_of = (None, 1, 0, 1)

    def sum_begin(q, g):
        b, two = bank_of[q], pl.ds(2 * g, 2)
        csend[q, g] = remote(part.at[b, two, other], c_recv.at[b, two], c_s.at[b, g], c_r.at[q - 1, g], mate)

    def sum_cross(q, g):
        b, two = bank_of[q], pl.ds(2 * g, 2)
        csend[q, g].wait_recv()
        part[b, two, own] = part[b, two, own] + c_recv[b, two]
        xsend[q, g] = remote(part.at[b, two, own], x_recv.at[q - 1, two], x_s.at[b, g], x_r.at[q - 1, g], far)

    def sum_share(q, g):
        b, two = bank_of[q], pl.ds(2 * g, 2)
        xsend[q, g].wait()
        part[b, two, own] = part[b, two, own] + x_recv[q - 1, two]
        asend[q, g] = remote(part.at[b, two, own], a_recv.at[b, two], a_s.at[b, g], a_r.at[q - 1, g], mate)

    def sum_end(q, g):
        b, two = bank_of[q], pl.ds(2 * g, 2)
        csend[q, g].wait_send()
        asend[q, g].wait()
        part[b, two, other] = a_recv[b, two]

    def grad_hidden(g):
        whole = cot[2 * g : 2 * g + 2].reshape(2 * TB, D)
        value = whole.astype(BF16)
        for i in range(2):
            gf[i, :, g * 256 : (g + 1) * 256] = whole[:, i * POS : (i + 1) * POS].T.astype(BF16)
        for n, width in TILES:
            gh[rows_of(g), n : n + width] = mm(value, wd[:, n : n + width], NN)

    def ffn_norm():
        for r in range(ROWS):
            m = mid[r]
            scale = lax.rsqrt(jnp.mean(m * m, axis=-1, keepdims=True) + EPS)
            aff[r * TB : (r + 1) * TB] = (m * scale * norm_two[...]).astype(BF16)

    def ffn_tiles(tiles):
        act = aff[...]
        for n, width in tiles:
            at = (slice(None), slice(n, n + width))
            gate = mm(act, wg[at], NN)
            upv = mm(act, wu[at], NN)
            sig = jax.nn.sigmoid(gate)
            silu = gate * sig
            grad = gh[at]
            hid[at] = (silu * upv).astype(BF16)
            gu[at] = (grad * silu).astype(BF16)
            gg[at] = (grad * upv * sig * (1.0 + gate * (1.0 - sig))).astype(BF16)

    def ffn_back(g):
        partial = mm(gg[rows_of(g)], wg[...], NT) + mm(gu[rows_of(g)], wu[...], NT)
        part[1, 2 * g : 2 * g + 2] = partial.reshape(2, TB, D)
        sum_begin(1, g)

    def ffn_out(g):
        partial = mm(hid[rows_of(g)], wd[...], NT)
        part[1, 2 * g : 2 * g + 2] = partial.reshape(2, TB, D)
        sum_begin(3, g)

    def product(slot, left, right, n, width):
        @pl.loop(0, 4)
        def _(i):
            columns = pl.ds(pl.multiple_of(i * 256, 256), 256)
            value = mm(left[:, columns], right, TN)
            value = value.reshape(4, 2, 32, width)
            grads[slot, i, :, :, :, n : n + width] = value

    def product_down(tiles):
        for n, width in tiles:
            right = hid[:, n : n + width]
            for i in range(2):
                value = mm(gf[i], right, NN).reshape(2, 4, 2, 32, width)
                grads[0, 2 * i : 2 * i + 2, :, :, :, n : n + width] = value

    def product_out():
        right = wg[0:POS, 0:CH]
        for i in range(4):
            left = gf[i // 2, :, i % 2 * 256 : (i % 2 + 1) * 256]
            grads_out[i] = mm(left, right, TN).reshape(4, 2, 32, CH)

    outs = []

    def leave(src, dst):
        outs.append(pltpu.make_async_copy(src, dst, out_sem.at[len(outs)]))
        outs[-1].start()

    place = (y, z)

    def slot_of(job):
        return 2 if job == 4 else job % 2

    def block_of(job):
        slot, at, n, deep = JOBS[job]
        return slot, pl.ds(at, n), pl.ds(0, deep), deep

    def sems_of(job, p, k):
        if k >= 6:
            return split_s.at[p, k - 6], split_r.at[p, k - 6]
        return s1_s.at[slot_of(job), p, k], s1_r.at[slot_of(job), p, k]

    def chunk(job, p, j, half=None, columns=None):
        slot, every, rows, deep = block_of(job)
        columns = every if columns is None else columns
        cut = pl.ds(0, 4) if half is None else pl.ds(2 * half, 2)
        if deep != 32:
            rows = pl.ds(deep * p, deep)
            return grads_out.at[j, cut, l, rows] if p == 0 else grads_out.at[cut, j, l, rows]
        if p == 0:
            return grads.at[slot, j, cut, 0, rows, columns]
        return grads.at[slot, cut, j, 1, rows, columns]

    pair = []

    def pair_begin():
        pair.append(remote(grads_out.at[:, :, 1 - l], paired, p_s.at[0], p_r.at[0], across))

    def pair_end():
        pair[0].wait()

        @pl.loop(0, 4)
        def _(i):
            grads_out[i, :, l] = grads_out[i, :, l] + paired[i]

    first = {}

    def ring_begin(job, cut=None):
        slot, columns, rows, _ = block_of(job)
        columns, base = (columns, 0) if cut is None else (pl.ds(*cut), 6 if cut[0] else 0)
        for p in range(2):
            i = place[p]
            if job in (2, 3):
                pl.semaphore_wait(credit.at[slot, p, 0], 1)
                pl.semaphore_wait(credit.at[slot, p, 1], 1)
            copies = first.setdefault((job, p), {})
            for k, half, to in ((0, 0, plus[p]), (1, 1, minus[p])):
                copies[base + k] = remote(
                    chunk(job, p, up(i, 2), half, columns), rel1.at[slot, p, k, :, rows, columns],
                    *sems_of(job, p, base + k), to,
                )

    def ring_fill(job, cut=None):
        slot, columns, rows, _ = block_of(job)
        columns, base = (columns, 2) if cut is None else (pl.ds(*cut), 8 if cut[0] else 2)
        for p in range(2):
            i = place[p]
            for k, half, to in ((0, 1, plus[p]), (1, 0, minus[p])):
                first[job, p][base + k] = remote(
                    chunk(job, p, up(i, 1 + 2 * k), half, columns),
                    fin1.at[slot, p, k, pl.ds(2 * half, 2), rows, columns],
                    *sems_of(job, p, base + k), to,
                )

    def ring_relay(job):
        slot, columns, rows, _ = block_of(job)
        for p in range(2):
            i = place[p]
            copies = first[job, p]
            for k, j, half, to in ((0, up(i), 0, plus[p]), (1, up(i, 3), 1, minus[p])):
                copies[k].wait_recv()
                if 6 + k in copies:
                    copies[6 + k].wait_recv()
                target = chunk(job, p, j, half)
                for m in range(2):
                    target[m] = target[m] + rel1[slot, p, k, m, rows, columns]
                copies[4 + k] = remote(
                    target, fin1.at[slot, p, k, pl.ds(2 * half, 2), rows, columns],
                    s1_s.at[slot_of(job), p, 4 + k], s1_r.at[slot_of(job), p, 4 + k], to,
                )

    second = {}

    def piece(job, p, j, half=None):
        slot, columns, _, deep = block_of(job)
        row = (slot * 2 + p) * 128 + j * 32
        if half is None:
            return gh.at[pl.ds(pl.multiple_of(row, 32), deep), columns]
        return gh.at[pl.ds(pl.multiple_of(row + deep // 2 * half, 8), deep // 2), columns]

    def ring_turn(job):
        slot, columns, rows, deep = block_of(job)
        at, cut = min(job, 3), (pl.ds(0, deep // 2), pl.ds(deep // 2, deep // 2))
        for p in range(2):
            for k in (2, 3, 8, 9, 4, 5):
                if k in first[job, p]:
                    first[job, p][k].wait_recv()
            mine = chunk(job, p, place[p])

            @pl.loop(0, 4)
            def _(m):
                to = pl.ds(pl.multiple_of((slot * 2 + p) * 128 + m * 32, 32), deep)
                gh[to, columns] = (
                    mine[m] + fin1[slot, p, 0, m, rows, columns] + fin1[slot, p, 1, m, rows, columns]
                )

            if job < 2:
                pl.semaphore_signal(credit.at[slot, p, 0], inc=1, device_id=minus[p], device_id_type=MESH)
                pl.semaphore_signal(credit.at[slot, p, 1], inc=1, device_id=plus[p], device_id_type=MESH)
            i = place[1 - p]
            sems = lambda k: (s2_s.at[slot_of(job), p, k], s2_r.at[job, p, k])
            a, b = plus[1 - p], minus[1 - p]
            if job >= 3:
                beyond = dev(z=up(z, 2)) if p == 0 else dev(y=up(y, 2))
                second[job, p] = {
                    0: remote(piece(job, p, up(i, 2), 0), rel2.at[at, p, 0, cut[0], columns], *sems(0), beyond),
                    1: remote(piece(job, p, up(i, 2), 1), rel2.at[at, p, 1, cut[0], columns], *sems(1), beyond),
                    2: remote(piece(job, p, up(i)), fin2.at[at, p, 0, rows, columns], *sems(2), a),
                    3: remote(piece(job, p, up(i, 3)), fin2.at[at, p, 1, rows, columns], *sems(3), b),
                }
                continue
            second[job, p] = {
                0: remote(piece(job, p, up(i, 2), 0), rel2.at[at, p, 0, cut[0], columns], *sems(0), a),
                1: remote(piece(job, p, up(i, 2), 1), rel2.at[at, p, 1, cut[0], columns], *sems(1), b),
                2: remote(piece(job, p, up(i), 1), fin2.at[at, p, 0, cut[1], columns], *sems(2), a),
                3: remote(piece(job, p, up(i, 3), 0), fin2.at[at, p, 1, cut[0], columns], *sems(3), b),
            }

    def ring_relay_two(job):
        _, columns, _, deep = block_of(job)
        at, cut = min(job, 3), (pl.ds(0, deep // 2), pl.ds(deep // 2, deep // 2))
        for p in range(2):
            i = place[1 - p]
            copies = second[job, p]
            for k, j, half, to in ((0, up(i), 0, plus[1 - p]), (1, up(i, 3), 1, minus[1 - p])):
                copies[k].wait_recv()
                target = piece(job, p, j, half)
                target[...] = target[...] + rel2[at, p, k, cut[0], columns]
                copies[4 + k] = remote(
                    target, fin2.at[at, p, k, cut[half], columns],
                    s2_s.at[slot_of(job), p, 4 + k], s2_r.at[job, p, 4 + k], to,
                )

    third = {}

    def ring_cross(job):
        _, columns, rows, deep = block_of(job)
        at = min(job, 3)
        for p in range(2):
            for k in (2, 3, 0, 1) if job >= 3 else (2, 3, 4, 5):
                second[job, p][k].wait_recv()
            total = (
                piece(job, p, place[1 - p])[...]
                + fin2[at, p, 0, rows, columns]
                + fin2[at, p, 1, rows, columns]
            )
            if job >= 3:
                low = pl.ds(0, deep // 2)
                total += jnp.concatenate([rel2[at, p, 0, low, columns], rel2[at, p, 1, low, columns]], axis=0)
            if deep == 32:
                fin2[at, p, 0, :, columns] = total
            else:
                paired[0, 0, p * deep : (p + 1) * deep] = total
        if deep != 32:
            leave(paired.at[0, 0], o_out)
        else:
            third[job] = remote(
                fin2.at[at, 1 - l, 0, :, columns], last.at[at, :, columns], s3_s.at[job], s3_r.at[job], across
            )

    def ring_end(job):
        columns = block_of(job)[1]
        third[job].wait()
        last[job, :, columns] = fin2[job, l, 0, :, columns] + last[job, :, columns]
        if job < 3:
            leave(last.at[job], (o_down, o_gate, o_up)[job])
        else:
            for j in range(3):
                leave(last.at[job, :, pl.ds(j * CH, CH)], o_in.at[j])

    def ring_sent(job, copies):
        for p in range(2):
            for copy in copies[job, p].values():
                copy.wait_send()

    back = {}

    def mixer_back(g):
        for r in (2 * g, 2 * g + 1):
            rows = pl.ds(r * TB, TB)
            m, grad = mid[r], part[1, r]
            scale = lax.rsqrt(jnp.mean(m * m, axis=-1, keepdims=True) + EPS)
            small[0:1] += jnp.sum(grad * m * scale, axis=0, keepdims=True)
            weighted = grad * norm_two[...]
            total = (
                cot[r]
                + scale * weighted
                - m * (scale * scale * scale) * jnp.mean(weighted * m, axis=-1, keepdims=True)
            )
            cot[r] = total
            for i in range(2):
                gf[i, rows] = total[:, i * POS : (i + 1) * POS].astype(BF16)
        gmix = mm(gf[0, rows_of(g)], wout[0:POS], NN) + mm(gf[1, rows_of(g)], wout[POS:], NN)
        for k in range(2):
            r = 2 * g + k
            rows = pl.ds(r * TB, TB)
            value = gmix[k * TB : (k + 1) * TB]
            total = conv(r, 0, TB)
            gg[rows, CH : 2 * CH] = (value * total).astype(BF16)
            wg[rows, 0:CH] = (proj[1, rows] * total).astype(BF16)
            gce[r, 0:TB] = value * proj[1, rows]
            sbuf[r] = gce[r, 0:8] * keep[r]
        two = pl.ds(2 * g, 2)
        back[g] = remote(sbuf.at[two], hb.at[two], h_s.at[g], h_r.at[g], previous)

    def mixer_back_in(g):
        back[g].wait()
        for r in (2 * g, 2 * g + 1):
            rows = pl.ds(r * TB, TB)
            gce[r, TB:] = hb[r]
            value = gce[r, 0:TB]
            for k in range(3):
                small[2 + k : 3 + k, 0:CH] += jnp.sum(
                    value * bxe[r, 6 + k : 6 + k + TB], axis=0, keepdims=True
                )
            gbx = w_conv[2:3] * value + w_conv[1:2] * gce[r, 1 : 1 + TB] + w_conv[0:1] * gce[r, 2 : 2 + TB]
            gg[rows, 0:CH] = (gbx * proj[2, rows]).astype(BF16)
            gg[rows, 2 * CH : 3 * CH] = (gbx * proj[0, rows]).astype(BF16)
        partial = mm(gg[rows_of(g), 0:CH], win[0], NT)
        for j in (1, 2):
            partial += mm(gg[rows_of(g), j * CH : (j + 1) * CH], win[j], NT)
        part[0, 2 * g : 2 * g + 2] = partial.reshape(2, TB, D)
        sum_begin(2, g)

    def tokens_out(r):
        t, grad = tok[r], part[0, r]
        scale = lax.rsqrt(jnp.mean(t * t, axis=-1, keepdims=True) + EPS)
        small[1:2] += jnp.sum(grad * t * scale, axis=0, keepdims=True)
        weighted = grad * norm_one[...]
        cot[r] = (
            cot[r]
            + scale * weighted
            - t * (scale * scale * scale) * jnp.mean(weighted * t, axis=-1, keepdims=True)
        )
        leave(cot.at[r], grad_tokens.at[r])

    def result_out(r):
        mid[r] = mid[r] + part[1, r]
        leave(mid.at[r], result.at[r])

    reduced = {}

    def small_begin(stage):
        at, peers = (
            (l, [across]),
            (y, [dev(y=up(y, k)) for k in (1, 2, 3)]),
            (z, [dev(z=up(z, k)) for k in (1, 2, 3)]),
        )[stage]
        ar[stage, at] = small[...]
        reduced[stage] = [
            remote(small, ar.at[stage, at], ar_s.at[k], ar_r.at[stage, at], to)
            for k, to in enumerate(peers)
        ]

    def small_end(stage):
        at, count = ((l, 2), (y, 4), (z, 4))[stage]
        for k, copy in enumerate(reduced[stage]):
            copy.wait_send()
            there = (at + k + 1) % count
            pltpu.make_async_remote_copy(
                src_ref=small, dst_ref=ar.at[stage, there], send_sem=ar_s.at[k],
                recv_sem=ar_r.at[stage, there], device_id=mate, device_id_type=MESH,
            ).wait_recv()
        total = ar[stage, 0] + ar[stage, 1]
        for k in range(2, count):
            total += ar[stage, k]
        small[...] = total

    loads["wout"].wait()
    weight_begin()
    loads["tok"].wait()
    loads["win"].wait()
    mixer_in(0)
    pl.semaphore_wait(barrier, len(partners))
    weight_far()
    mixer_out(0)
    mixer_in(1)
    send_halo()
    mixer_out(1)
    weight_first()
    loads["cot"].wait()
    loads["wd"].wait()
    grad_hidden(0)
    grad_hidden(1)
    weight_second()
    mixer_edge()
    mix_pass(0)
    weight_near()
    for k in range(3):
        mix_near(k)
    branch(h, tok)
    mix_pass(1)
    weight_third()
    mix_pass(2)
    loads["wg"].wait()
    loads["wu"].wait()
    for k in range(3):
        mix_end(k)
    weight_end()
    branch(1 - h, mid)
    ffn_norm()
    for tile in TILES[:2]:
        ffn_tiles([tile])
        product_down([tile])
    ring_begin(0, (0, 512))
    ffn_tiles(TILES[2:])
    product_down(TILES[2:])
    ring_begin(0, (512, 640))
    ring_fill(0)
    ffn_back(0)
    ffn_back(1)
    sum_cross(1, 0)
    sum_cross(1, 1)
    product(1, aff, gg[...], 0, HID)
    ring_relay(0)
    ring_begin(1)
    ring_fill(1)
    sum_share(1, 0)
    sum_end(1, 0)
    mixer_back(0)
    ring_turn(0)
    ring_sent(0, first)
    product(0, aff, gu[...], 0, HID)
    ffn_out(0)
    sum_cross(3, 0)
    ring_relay(1)
    ring_begin(2)
    sum_share(1, 1)
    sum_end(1, 1)
    mixer_back(1)
    product_out()
    pair_begin()
    mixer_back_in(0)
    ring_fill(2)
    ffn_out(1)
    sum_cross(2, 0)
    ring_relay_two(0)
    mixer_back_in(1)
    ring_turn(1)
    ring_sent(1, first)
    sum_cross(2, 1)
    for g in (0, 1):
        aff[rows_of(g)] = normed(g)
    product(1, aff, gg[:, 0 : 3 * CH], 0, 3 * CH)
    ring_begin(3)
    ring_relay(2)
    pair_end()
    ring_begin(4)
    ring_cross(0)
    sum_share(3, 0)
    sum_end(3, 0)
    result_out(0)
    result_out(1)
    ring_relay_two(1)
    ring_fill(3)
    ring_fill(4)
    sum_share(2, 0)
    sum_cross(3, 1)
    ring_sent(0, second)
    ring_relay(3)
    sum_end(2, 0)
    for r in (0, 1):
        tokens_out(r)
    ring_turn(2)
    ring_relay(4)
    sum_share(2, 1)
    sum_end(2, 1)
    for r in (2, 3):
        tokens_out(r)
    small_begin(0)
    ring_cross(1)
    ring_sent(1, second)
    ring_turn(3)
    ring_relay_two(2)
    ring_turn(4)
    small_end(0)
    small_begin(1)
    ring_cross(3)
    small_end(1)
    small_begin(2)
    ring_cross(2)
    ring_cross(4)
    sum_share(3, 1)
    sum_end(3, 1)
    for r in (2, 3):
        result_out(r)
    ring_end(0)
    ring_end(1)
    small_end(2)
    leave(small, o_small)
    for job in range(2, 5):
        ring_sent(job, first)
        ring_sent(job, second)
    ring_end(3)
    ring_end(2)
    for copy in outs:
        copy.wait()


def finish(*refs):
    ins, outs, held, sem = refs[:8], refs[8:18], refs[18:28], refs[28]
    parts = [(k, r) for r in range(ROWS) for k in range(2)] + [(k, None) for k in range(2, 10)]

    def move(way, n):
        k, r = parts[n]
        src, dst = ((ins, held), (held, outs))[way]
        if r is None:
            return pltpu.make_async_copy(src[k], dst[k], sem.at[way, n])
        return pltpu.make_async_copy(src[k].at[r], dst[k].at[r], sem.at[way, n])

    incoming = [move(0, n) for n in range(13)]
    for copy in incoming:
        copy.start()
    small = ins[7]
    held[7][...] = small[1]
    held[8][...] = small[0]
    held[9][...] = small[2:5, 0:CH]
    outgoing = [move(1, n) for n in range(13, 16)]
    for copy in outgoing:
        copy.start()
    for n, copy in enumerate(incoming):
        copy.wait()
        outgoing.append(move(1, n))
        outgoing[-1].start()
    for copy in outgoing:
        copy.wait()


def on_device(
    tokens, start_flags, norm_one, w_in, w_conv, w_out, norm_two, w_gate, w_up, w_down, cotangent
):
    any_spec = pl.BlockSpec(memory_space=pl.ANY)
    vmem = pl.BlockSpec(memory_space=pltpu.VMEM)
    dma = pltpu.SemaphoreType.DMA
    shape = jax.ShapeDtypeStruct
    outs = pl.pallas_call(
        kernel,
        out_shape=(
            shape((ROWS, TB, D), F32),
            shape((ROWS, TB, D), F32),
            shape((3, 32, CH), F32),
            shape((32, CH), F32),
            shape((32, HID), F32),
            shape((32, HID), F32),
            shape((32, HID), F32),
            shape((8, D), F32),
        ),
        in_specs=[pl.BlockSpec(memory_space=pltpu.SMEM)] + [any_spec] * 7 + [vmem] * 3,
        out_specs=(any_spec,) * 8,
        scratch_shapes=[
            pltpu.VMEM((ROWS, TB, D), F32),
            pltpu.VMEM((ROWS, TB, D), F32),
            pltpu.VMEM((3, D, CH), BF16),
            pltpu.VMEM((D, CH), BF16),
            pltpu.VMEM((D, HID), BF16),
            pltpu.VMEM((D, HID), BF16),
            pltpu.VMEM((D, HID), BF16),
            pltpu.VMEM((3, POS, CH), F32),
            pltpu.VMEM((ROWS, TB + 8, CH), F32),
            pltpu.VMEM((ROWS, TB + 8, CH), F32),
            pltpu.VMEM((ROWS, TB, D), F32),
            pltpu.VMEM((POS, D), BF16),
            pltpu.VMEM((POS, HID), BF16),
            pltpu.VMEM((POS, HID), BF16),
            pltpu.VMEM((POS, HID), BF16),
            pltpu.VMEM((2, POS, POS), BF16),
            pltpu.VMEM((POS, HID), F32),
                pltpu.VMEM((ROWS, 8, CH), F32),
            pltpu.VMEM((ROWS, 8, CH), F32),
            pltpu.VMEM((ROWS, 8, CH), F32),
            pltpu.VMEM((2, ROWS, TB, D), F32),
            pltpu.VMEM((2, ROWS, HALF, D), F32),
            pltpu.VMEM((3, ROWS, HALF, D), F32),
            pltpu.VMEM((2, ROWS, HALF, D), F32),
            pltpu.VMEM((2, 4, 4, 2, 32, HID), F32),
            pltpu.VMEM((2, 2, 2, 2, 32, HID), F32),
            pltpu.VMEM((2, 2, 2, 4, 32, HID), F32),
            pltpu.VMEM((4, 2, 2, 16, HID), F32),
            pltpu.VMEM((4, 2, 2, 32, HID), F32),
            pltpu.VMEM((4, 32, HID), F32),
            pltpu.VMEM((4, 4, 2, 32, CH), F32),
            pltpu.VMEM((4, 4, 32, CH), F32),
            pltpu.VMEM((8, D), F32),
            pltpu.VMEM((3, 4, 8, D), F32),
            dma((7,)),
            dma((16,)),
            dma((3, 3)),
            dma((3, 3)),
            dma((22,)),
            dma((22,)),
            dma((3,)),
            dma((3,)),
            dma((2, 2)),
            dma((3, 2)),
            dma((2, 2)),
            dma((3, 2)),
            dma((2, 2)),
            dma((3, 2)),
            dma((3, 2, 6)),
            dma((3, 2, 6)),
            dma((2, 4)),
            dma((2, 4)),
            dma((3, 2, 6)),
            dma((5, 2, 6)),
            dma((4,)),
            dma((4,)),
            dma((1,)),
            dma((1,)),
            dma((3,)),
            dma((3, 4)),
            pltpu.SemaphoreType.REGULAR((2, 2, 2)),
        ],
        compiler_params=pltpu.CompilerParams(
            collective_id=0, has_side_effects=True, vmem_limit_bytes=63 * 2**20
        ),
        name="block",
    )(
        start_flags.T, tokens, cotangent, w_in, w_out, w_gate, w_up, w_down,
        norm_one.reshape(1, D), norm_two.reshape(1, D), w_conv,
    )
    result, grad_tokens, g_in, g_out, g_gate, g_up, g_down, one, two, taps = pl.pallas_call(
        finish,
        out_shape=tuple(shape(o.shape, F32) for o in outs[:2])
        + (
            shape((3, 32, CH), F32),
            shape((32, CH), F32),
            shape((32, HID), F32),
            shape((32, HID), F32),
            shape((32, HID), F32),
            shape((D,), F32),
            shape((D,), F32),
            shape((3, CH), F32),
        ),
        in_specs=[any_spec] * 7 + [vmem],
        out_specs=(any_spec,) * 10,
        scratch_shapes=[pltpu.VMEM(o.shape, F32) for o in outs[:7]]
        + [pltpu.VMEM(d, F32) for d in ((D,), (D,), (3, CH))]
        + [dma((2, 16))],
        compiler_params=pltpu.CompilerParams(vmem_limit_bytes=60 * 2**20),
        name="finish",
    )(*outs)
    return result, grad_tokens, one, g_in, taps, g_out, two, g_gate, g_up, g_down


def solution(mesh):
    return jax.shard_map(
        on_device,
        mesh=mesh,
        in_specs=(
            P(None, "seq", None),
            P(None, "seq"),
            P(),
            P(None, None, "wt"),
            P(None, "wt"),
            P(None, "wt"),
            P(),
            P(None, "wt"),
            P(None, "wt"),
            P(None, "wt"),
            P(None, "seq", None),
        ),
        out_specs=(
            P(None, "seq", None),
            P(None, "seq", None),
            P(),
            P(None, "seq", "wt"),
            P(None, "wt"),
            P("seq", "wt"),
            P(),
            P("seq", "wt"),
            P("seq", "wt"),
            P("seq", "wt"),
        ),
        check_vma=False,
    )
```

```python
import functools

import jax
import jax.numpy as jnp
from jax import lax
from jax.experimental import pallas as pl
from jax.experimental.pallas import tpu as pltpu
from jax.sharding import PartitionSpec as P

EPS = 1e-05
MESH = pl.DeviceIdType.MESH
F32 = jnp.float32
BF16 = jnp.bfloat16
NN = ((1,), (0,))
NT = ((1,), (1,))
TN = ((0,), (0,))

ROWS, TB, D, CH, HID = 4, 128, 1024, 256, 1152
POS = ROWS * TB
HALF = TB // 2
JOBS = (
    (0, 0, HID, 32),
    (1, 0, HID, 32),
    (0, 0, HID, 32),
    (1, 0, 3 * CH, 32),
    (1, 3 * CH, CH, 16),
)
TILES = ((0, 256), (256, 256), (512, 256), (768, 256), (1024, 128))


def mm(a, b, dims):
    return lax.dot_general(a, b, (dims, ((), ())), preferred_element_type=F32)


def kernel(
    flags, tokens, cotangent, w_in, w_out, w_gate, w_up, w_down, norm_one, norm_two, w_conv,
    result, grad_tokens, o_in, o_out, o_gate, o_up, o_down, o_small,
    tok, cot, win, wout, wg, wu, wd,
    proj, bxe, gce, mid, aff, hid, gg, gu, gf, gh, sbuf, hf, hb,
    part, c_recv, x_recv, a_recv,
    grads, rel1, fin1, rel2, fin2, last, grads_out, paired, small, ar,
    in_sem, out_sem, m_s, m_r, v_s, v_r, h_s, h_r, c_s, c_r, x_s, x_r, a_s, a_r,
    s1_s, s1_r, split_s, split_r, s2_s, s2_r, s3_s, s3_r, p_s, p_r, ar_s, ar_r, credit,
):
    s = lax.axis_index("seq")
    w = lax.axis_index("wt")
    y, z, l = s // 8, (s // 2) % 4, s % 2
    h, c = w // 2, w % 2

    def dev(y=y, z=z, l=l, h=h, c=c):
        return ((y * 4 + z) * 2 + l, h * 2 + c)

    def up(v, by=1):
        return (v + by) % 4

    plus = (dev(y=up(y)), dev(z=up(z)))
    minus = (dev(y=up(y, 3)), dev(z=up(z, 3)))
    across = dev(l=1 - l)
    far = dev(h=1 - h)
    mate = dev(c=1 - c)
    following = ((s + 1) % 32, w)
    previous = ((s + 31) % 32, w)

    def remote(src, dst, send, recv, to):
        copy = pltpu.make_async_remote_copy(
            src_ref=src, dst_ref=dst, send_sem=send, recv_sem=recv, device_id=to, device_id_type=MESH
        )
        copy.start()
        return copy

    loads = {}

    def load(name, src, dst):
        loads[name] = pltpu.make_async_copy(src, dst, in_sem.at[len(loads)])
        loads[name].start()

    load("wout", w_out, wout)
    load("tok", tokens, tok)
    load("win", w_in, win)
    load("cot", cotangent, cot)
    load("wd", w_down, wd)
    load("wg", w_gate, wg)
    load("wu", w_up, wu)

    barrier = pltpu.get_barrier_semaphore()
    partners = (
        plus + minus + (dev(y=up(y, 2)), dev(z=up(z, 2)), across, far, mate, following, previous)
    )
    for partner in partners:
        pl.semaphore_signal(barrier, inc=1, device_id=partner, device_id_type=MESH)

    small[...] = jnp.zeros_like(small)

    def rows_of(g):
        return pl.ds(g * 2 * TB, 2 * TB)

    keep = [1.0 - (flags[0, r] == 1).astype(F32) for r in range(ROWS)]

    halo = {}

    def normed(g):
        t = tok[2 * g : 2 * g + 2].reshape(2 * TB, D)
        scale = lax.rsqrt(jnp.mean(t * t, axis=-1, keepdims=True) + EPS)
        return (t * scale * norm_one[...]).astype(BF16)

    def mixer_in(g):
        act = normed(g)
        for j in range(3):
            proj[j, rows_of(g)] = mm(act, win[j], NN)
        bx = proj[0, rows_of(g)] * proj[2, rows_of(g)]
        for k in range(2):
            bxe[2 * g + k, 8:] = bx[k * TB : (k + 1) * TB]

    def send_halo():
        halo[0] = remote(bxe.at[:, pl.ds(TB, 8)], hf, h_s.at[2], h_r.at[2], following)

    mine = pl.ds(pl.multiple_of(w * CH, CH), CH)
    theirs = pl.ds(pl.multiple_of(((1 - h) * 2 + c) * CH, CH), CH)
    weight = {}

    def weight_begin():
        @pl.loop(0, 4)
        def _(i):
            rows = pl.ds(pl.multiple_of(i * 256, 256), 256)
            grads[1, i, :, :, :, mine] = wout[rows].astype(F32).reshape(4, 2, 32, CH)

    def weight_far():
        block = grads.at[1, y, z, :, :, mine]
        weight["far"] = remote(block, block, v_s.at[0], v_r.at[0], far)
        block = grads.at[1, :, :, :, :, mine]
        weight["mate"] = remote(block, block, v_s.at[1], v_r.at[1], mate)

    def weight_first():
        weight["far"].wait_recv()
        for p in range(2):
            for k in (1, 2, 3):
                to = dev(y=up(y, k)) if p == 0 else dev(z=up(z, k))
                block = grads.at[1, y, z, p, :, theirs]
                weight["first", p, k] = remote(
                    block, block, v_s.at[1 + p * 3 + k], v_r.at[1 + p * 3 + k], to
                )

    def weight_row(p, j):
        return grads.at[1, :, j, 0, :, theirs] if p == 0 else grads.at[1, j, :, 1, :, theirs]

    def weight_pass(p, k):
        block = weight_row(p, up((z, y)[p], 4 - k))
        weight["pass", p, k] = remote(
            block, block, v_s.at[14 + p * 4 + k], v_r.at[14 + p * 4 + k], mate
        )

    def weight_second():
        for p in range(2):
            for k in (1, 2, 3):
                weight["first", p, k].wait_recv()
        for p in range(2):
            for k in (1, 2, 3):
                to = dev(z=up(z, k)) if p == 0 else dev(y=up(y, k))
                block = weight_row(p, (z, y)[p])
                weight["second", p, k] = remote(
                    block, block, v_s.at[7 + p * 3 + k], v_r.at[7 + p * 3 + k], to
                )
        for p in range(2):
            weight_pass(p, 0)

    def weight_third():
        for k in (1, 3, 2):
            for p in range(2):
                weight["second", p, k].wait_recv()
                weight_pass(p, k)

    def weight_near():
        weight["mate"].wait()

    def weight_end():
        weight["far"].wait_send()
        for p in range(2):
            for k in (1, 2, 3):
                weight["first", p, k].wait_send()
                weight["second", p, k].wait_send()
            for k in range(4):
                weight["pass", p, k].wait()

    mix = {}

    def mix_block(k, columns):
        if k < 2:
            return part.at[0, pl.ds(2 * k, 2), pl.ds(8, TB - 8), columns]
        return part.at[0, :, pl.ds(0, 8), columns]

    def mix_send(k):
        block = mix_block(k, mine)
        mix["far", k] = remote(block, block, m_s.at[0, k], m_r.at[0, k], far)
        mix["mate", k] = remote(block, block, m_s.at[1, k], m_r.at[1, k], mate)

    def mix_pass(k):
        mix["far", k].wait_recv()
        block = mix_block(k, theirs)
        mix["pass", k] = remote(block, block, m_s.at[2, k], m_r.at[2, k], mate)

    def mix_near(k):
        mix["mate", k].wait()

    def mix_end(k):
        mix["far", k].wait_send()
        mix["pass", k].wait()

    def conv(r, at, count):
        return (
            w_conv[0:1] * bxe[r, at + 6 : at + 6 + count]
            + w_conv[1:2] * bxe[r, at + 7 : at + 7 + count]
            + w_conv[2:3] * bxe[r, at + 8 : at + 8 + count]
        )

    def taps(r, at, count):
        total = conv(r, at, count)
        rows = pl.ds(r * TB + at, count)
        part[0, r, at : at + count, mine] = (proj[1, rows] * total).astype(BF16).astype(F32)

    def mixer_out(g):
        for r in (2 * g, 2 * g + 1):
            taps(r, 8, TB - 8)
        mix_send(g)

    def mixer_edge():
        halo[0].wait()
        for r in range(4):
            bxe[r, 0:8] = hf[r] * keep[r]
            taps(r, 0, 8)
        mix_send(2)

    def branch(chip, start):
        half = pl.ds(pl.multiple_of(chip * 2 * CH, 2 * CH), 2 * CH)
        left = part[0, :, :, half].reshape(POS, 2 * CH).astype(BF16)
        for i in range(4):
            right = grads[1, i, :, :, :, half].reshape(256, 2 * CH).astype(BF16)
            columns = pl.ds(i * 256, 256)
            mid[:, :, columns] = start[:, :, columns] + mm(left, right, NT).reshape(ROWS, TB, 256)

    csend, xsend, asend = {}, {}, {}
    own = pl.ds(pl.multiple_of(c * HALF, HALF), HALF)
    other = pl.ds(pl.multiple_of((1 - c) * HALF, HALF), HALF)
    bank_of = (None, 1, 0, 1)

    def sum_begin(q, g):
        b, two = bank_of[q], pl.ds(2 * g, 2)
        csend[q, g] = remote(part.at[b, two, other], c_recv.at[b, two], c_s.at[b, g], c_r.at[q - 1, g], mate)

    def sum_cross(q, g):
        b, two = bank_of[q], pl.ds(2 * g, 2)
        csend[q, g].wait_recv()
        part[b, two, own] = part[b, two, own] + c_recv[b, two]
        xsend[q, g] = remote(part.at[b, two, own], x_recv.at[q - 1, two], x_s.at[b, g], x_r.at[q - 1, g], far)

    def sum_share(q, g):
        b, two = bank_of[q], pl.ds(2 * g, 2)
        xsend[q, g].wait()
        part[b, two, own] = part[b, two, own] + x_recv[q - 1, two]
        asend[q, g] = remote(part.at[b, two, own], a_recv.at[b, two], a_s.at[b, g], a_r.at[q - 1, g], mate)

    def sum_end(q, g):
        b, two = bank_of[q], pl.ds(2 * g, 2)
        csend[q, g].wait_send()
        asend[q, g].wait()
        part[b, two, other] = a_recv[b, two]

    def grad_hidden(g):
        whole = cot[2 * g : 2 * g + 2].reshape(2 * TB, D)
        value = whole.astype(BF16)
        for i in range(2):
            gf[i, :, g * 256 : (g + 1) * 256] = whole[:, i * POS : (i + 1) * POS].T.astype(BF16)
        for n, width in TILES:
            gh[rows_of(g), n : n + width] = mm(value, wd[:, n : n + width], NN)

    def ffn_norm():
        for r in range(ROWS):
            m = mid[r]
            scale = lax.rsqrt(jnp.mean(m * m, axis=-1, keepdims=True) + EPS)
            aff[r * TB : (r + 1) * TB] = (m * scale * norm_two[...]).astype(BF16)

    def ffn_tiles(tiles):
        act = aff[...]
        for n, width in tiles:
            at = (slice(None), slice(n, n + width))
            gate = mm(act, wg[at], NN)
            upv = mm(act, wu[at], NN)
            sig = jax.nn.sigmoid(gate)
            silu = gate * sig
            grad = gh[at]
            hid[at] = (silu * upv).astype(BF16)
            gu[at] = (grad * silu).astype(BF16)
            gg[at] = (grad * upv * sig * (1.0 + gate * (1.0 - sig))).astype(BF16)

    def ffn_back(g):
        partial = mm(gg[rows_of(g)], wg[...], NT) + mm(gu[rows_of(g)], wu[...], NT)
        part[1, 2 * g : 2 * g + 2] = partial.reshape(2, TB, D)
        sum_begin(1, g)

    def ffn_out(g):
        partial = mm(hid[rows_of(g)], wd[...], NT)
        part[1, 2 * g : 2 * g + 2] = partial.reshape(2, TB, D)
        sum_begin(3, g)

    def product(slot, left, right, n, width):
        @pl.loop(0, 4)
        def _(i):
            columns = pl.ds(pl.multiple_of(i * 256, 256), 256)
            value = mm(left[:, columns], right, TN)
            value = value.reshape(4, 2, 32, width)
            grads[slot, i, :, :, :, n : n + width] = value

    def product_down(tiles):
        for n, width in tiles:
            right = hid[:, n : n + width]
            for i in range(2):
                value = mm(gf[i], right, NN).reshape(2, 4, 2, 32, width)
                grads[0, 2 * i : 2 * i + 2, :, :, :, n : n + width] = value

    def product_out():
        right = wg[0:POS, 0:CH]
        for i in range(4):
            left = gf[i // 2, :, i % 2 * 256 : (i % 2 + 1) * 256]
            grads_out[i] = mm(left, right, TN).reshape(4, 2, 32, CH)

    outs = []

    def leave(src, dst):
        outs.append(pltpu.make_async_copy(src, dst, out_sem.at[len(outs)]))
        outs[-1].start()

    place = (y, z)

    def slot_of(job):
        return 2 if job == 4 else job % 2

    def block_of(job):
        slot, at, n, deep = JOBS[job]
        return slot, pl.ds(at, n), pl.ds(0, deep), deep

    def sems_of(job, p, k):
        if k >= 6:
            return split_s.at[p, k - 6], split_r.at[p, k - 6]
        return s1_s.at[slot_of(job), p, k], s1_r.at[slot_of(job), p, k]

    def chunk(job, p, j, half=None, columns=None):
        slot, every, rows, deep = block_of(job)
        columns = every if columns is None else columns
        cut = pl.ds(0, 4) if half is None else pl.ds(2 * half, 2)
        if deep != 32:
            rows = pl.ds(deep * p, deep)
            return grads_out.at[j, cut, l, rows] if p == 0 else grads_out.at[cut, j, l, rows]
        if p == 0:
            return grads.at[slot, j, cut, 0, rows, columns]
        return grads.at[slot, cut, j, 1, rows, columns]

    pair = []

    def pair_begin():
        pair.append(remote(grads_out.at[:, :, 1 - l], paired, p_s.at[0], p_r.at[0], across))

    def pair_end():
        pair[0].wait()

        @pl.loop(0, 4)
        def _(i):
            grads_out[i, :, l] = grads_out[i, :, l] + paired[i]

    first = {}

    def ring_begin(job, cut=None):
        slot, columns, rows, _ = block_of(job)
        columns, base = (columns, 0) if cut is None else (pl.ds(*cut), 6 if cut[0] else 0)
        for p in range(2):
            i = place[p]
            if job in (2, 3):
                pl.semaphore_wait(credit.at[slot, p, 0], 1)
                pl.semaphore_wait(credit.at[slot, p, 1], 1)
            copies = first.setdefault((job, p), {})
            for k, half, to in ((0, 0, plus[p]), (1, 1, minus[p])):
                copies[base + k] = remote(
                    chunk(job, p, up(i, 2), half, columns), rel1.at[slot, p, k, :, rows, columns],
                    *sems_of(job, p, base + k), to,
                )

    def ring_fill(job, cut=None):
        slot, columns, rows, _ = block_of(job)
        columns, base = (columns, 2) if cut is None else (pl.ds(*cut), 8 if cut[0] else 2)
        for p in range(2):
            i = place[p]
            for k, half, to in ((0, 1, plus[p]), (1, 0, minus[p])):
                first[job, p][base + k] = remote(
                    chunk(job, p, up(i, 1 + 2 * k), half, columns),
                    fin1.at[slot, p, k, pl.ds(2 * half, 2), rows, columns],
                    *sems_of(job, p, base + k), to,
                )

    def ring_relay(job):
        slot, columns, rows, _ = block_of(job)
        for p in range(2):
            i = place[p]
            copies = first[job, p]
            for k, j, half, to in ((0, up(i), 0, plus[p]), (1, up(i, 3), 1, minus[p])):
                copies[k].wait_recv()
                if 6 + k in copies:
                    copies[6 + k].wait_recv()
                target = chunk(job, p, j, half)
                for m in range(2):
                    target[m] = target[m] + rel1[slot, p, k, m, rows, columns]
                copies[4 + k] = remote(
                    target, fin1.at[slot, p, k, pl.ds(2 * half, 2), rows, columns],
                    s1_s.at[slot_of(job), p, 4 + k], s1_r.at[slot_of(job), p, 4 + k], to,
                )

    second = {}

    def piece(job, p, j, half=None):
        slot, columns, _, deep = block_of(job)
        row = (slot * 2 + p) * 128 + j * 32
        if half is None:
            return gh.at[pl.ds(pl.multiple_of(row, 32), deep), columns]
        return gh.at[pl.ds(pl.multiple_of(row + deep // 2 * half, 8), deep // 2), columns]

    def ring_turn(job):
        slot, columns, rows, deep = block_of(job)
        at, cut = min(job, 3), (pl.ds(0, deep // 2), pl.ds(deep // 2, deep // 2))
        for p in range(2):
            for k in (2, 3, 8, 9, 4, 5):
                if k in first[job, p]:
                    first[job, p][k].wait_recv()
            mine = chunk(job, p, place[p])

            @pl.loop(0, 4)
            def _(m):
                to = pl.ds(pl.multiple_of((slot * 2 + p) * 128 + m * 32, 32), deep)
                gh[to, columns] = (
                    mine[m] + fin1[slot, p, 0, m, rows, columns] + fin1[slot, p, 1, m, rows, columns]
                )

            if job < 2:
                pl.semaphore_signal(credit.at[slot, p, 0], inc=1, device_id=minus[p], device_id_type=MESH)
                pl.semaphore_signal(credit.at[slot, p, 1], inc=1, device_id=plus[p], device_id_type=MESH)
            i = place[1 - p]
            sems = lambda k: (s2_s.at[slot_of(job), p, k], s2_r.at[job, p, k])
            a, b = plus[1 - p], minus[1 - p]
            if job >= 3:
                beyond = dev(z=up(z, 2)) if p == 0 else dev(y=up(y, 2))
                second[job, p] = {
                    0: remote(piece(job, p, up(i, 2), 0), rel2.at[at, p, 0, cut[0], columns], *sems(0), beyond),
                    1: remote(piece(job, p, up(i, 2), 1), rel2.at[at, p, 1, cut[0], columns], *sems(1), beyond),
                    2: remote(piece(job, p, up(i)), fin2.at[at, p, 0, rows, columns], *sems(2), a),
                    3: remote(piece(job, p, up(i, 3)), fin2.at[at, p, 1, rows, columns], *sems(3), b),
                }
                continue
            second[job, p] = {
                0: remote(piece(job, p, up(i, 2), 0), rel2.at[at, p, 0, cut[0], columns], *sems(0), a),
                1: remote(piece(job, p, up(i, 2), 1), rel2.at[at, p, 1, cut[0], columns], *sems(1), b),
                2: remote(piece(job, p, up(i), 1), fin2.at[at, p, 0, cut[1], columns], *sems(2), a),
                3: remote(piece(job, p, up(i, 3), 0), fin2.at[at, p, 1, cut[0], columns], *sems(3), b),
            }

    def ring_relay_two(job):
        _, columns, _, deep = block_of(job)
        at, cut = min(job, 3), (pl.ds(0, deep // 2), pl.ds(deep // 2, deep // 2))
        for p in range(2):
            i = place[1 - p]
            copies = second[job, p]
            for k, j, half, to in ((0, up(i), 0, plus[1 - p]), (1, up(i, 3), 1, minus[1 - p])):
                copies[k].wait_recv()
                target = piece(job, p, j, half)
                target[...] = target[...] + rel2[at, p, k, cut[0], columns]
                copies[4 + k] = remote(
                    target, fin2.at[at, p, k, cut[half], columns],
                    s2_s.at[slot_of(job), p, 4 + k], s2_r.at[job, p, 4 + k], to,
                )

    third = {}

    def ring_cross(job):
        _, columns, rows, deep = block_of(job)
        at = min(job, 3)
        for p in range(2):
            for k in (2, 3, 0, 1) if job >= 3 else (2, 3, 4, 5):
                second[job, p][k].wait_recv()
            total = (
                piece(job, p, place[1 - p])[...]
                + fin2[at, p, 0, rows, columns]
                + fin2[at, p, 1, rows, columns]
            )
            if job >= 3:
                low = pl.ds(0, deep // 2)
                total += jnp.concatenate([rel2[at, p, 0, low, columns], rel2[at, p, 1, low, columns]], axis=0)
            if deep == 32:
                fin2[at, p, 0, :, columns] = total
            else:
                paired[0, 0, p * deep : (p + 1) * deep] = total
        if deep != 32:
            leave(paired.at[0, 0], o_out)
        else:
            third[job] = remote(
                fin2.at[at, 1 - l, 0, :, columns], last.at[at, :, columns], s3_s.at[job], s3_r.at[job], across
            )

    def ring_end(job):
        columns = block_of(job)[1]
        third[job].wait()
        last[job, :, columns] = fin2[job, l, 0, :, columns] + last[job, :, columns]
        if job < 3:
            leave(last.at[job], (o_down, o_gate, o_up)[job])
        else:
            for j in range(3):
                leave(last.at[job, :, pl.ds(j * CH, CH)], o_in.at[j])

    def ring_sent(job, copies):
        for p in range(2):
            for copy in copies[job, p].values():
                copy.wait_send()

    back = {}

    def mixer_back(g):
        for r in (2 * g, 2 * g + 1):
            rows = pl.ds(r * TB, TB)
            m, grad = mid[r], part[1, r]
            scale = lax.rsqrt(jnp.mean(m * m, axis=-1, keepdims=True) + EPS)
            small[0:1] += jnp.sum(grad * m * scale, axis=0, keepdims=True)
            weighted = grad * norm_two[...]
            total = (
                cot[r]
                + scale * weighted
                - m * (scale * scale * scale) * jnp.mean(weighted * m, axis=-1, keepdims=True)
            )
            cot[r] = total
            for i in range(2):
                gf[i, rows] = total[:, i * POS : (i + 1) * POS].astype(BF16)
        gmix = mm(gf[0, rows_of(g)], wout[0:POS], NN) + mm(gf[1, rows_of(g)], wout[POS:], NN)
        for k in range(2):
            r = 2 * g + k
            rows = pl.ds(r * TB, TB)
            value = gmix[k * TB : (k + 1) * TB]
            total = conv(r, 0, TB)
            gg[rows, CH : 2 * CH] = (value * total).astype(BF16)
            wg[rows, 0:CH] = (proj[1, rows] * total).astype(BF16)
            gce[r, 0:TB] = value * proj[1, rows]
            sbuf[r] = gce[r, 0:8] * keep[r]
        two = pl.ds(2 * g, 2)
        back[g] = remote(sbuf.at[two], hb.at[two], h_s.at[g], h_r.at[g], previous)

    def mixer_back_in(g):
        back[g].wait()
        for r in (2 * g, 2 * g + 1):
            rows = pl.ds(r * TB, TB)
            gce[r, TB:] = hb[r]
            value = gce[r, 0:TB]
            for k in range(3):
                small[2 + k : 3 + k, 0:CH] += jnp.sum(
                    value * bxe[r, 6 + k : 6 + k + TB], axis=0, keepdims=True
                )
            gbx = w_conv[2:3] * value + w_conv[1:2] * gce[r, 1 : 1 + TB] + w_conv[0:1] * gce[r, 2 : 2 + TB]
            gg[rows, 0:CH] = (gbx * proj[2, rows]).astype(BF16)
            gg[rows, 2 * CH : 3 * CH] = (gbx * proj[0, rows]).astype(BF16)
        partial = mm(gg[rows_of(g), 0:CH], win[0], NT)
        for j in (1, 2):
            partial += mm(gg[rows_of(g), j * CH : (j + 1) * CH], win[j], NT)
        part[0, 2 * g : 2 * g + 2] = partial.reshape(2, TB, D)
        sum_begin(2, g)

    def tokens_out(r):
        t, grad = tok[r], part[0, r]
        scale = lax.rsqrt(jnp.mean(t * t, axis=-1, keepdims=True) + EPS)
        small[1:2] += jnp.sum(grad * t * scale, axis=0, keepdims=True)
        weighted = grad * norm_one[...]
        cot[r] = (
            cot[r]
            + scale * weighted
            - t * (scale * scale * scale) * jnp.mean(weighted * t, axis=-1, keepdims=True)
        )
        leave(cot.at[r], grad_tokens.at[r])

    def result_out(r):
        mid[r] = mid[r] + part[1, r]
        leave(mid.at[r], result.at[r])

    reduced = {}

    def small_begin(stage):
        at, peers = (
            (l, [across]),
            (y, [dev(y=up(y, k)) for k in (1, 2, 3)]),
            (z, [dev(z=up(z, k)) for k in (1, 2, 3)]),
        )[stage]
        ar[stage, at] = small[...]
        reduced[stage] = [
            remote(small, ar.at[stage, at], ar_s.at[k], ar_r.at[stage, at], to)
            for k, to in enumerate(peers)
        ]

    def small_end(stage):
        at, count = ((l, 2), (y, 4), (z, 4))[stage]
        for k, copy in enumerate(reduced[stage]):
            copy.wait_send()
            there = (at + k + 1) % count
            pltpu.make_async_remote_copy(
                src_ref=small, dst_ref=ar.at[stage, there], send_sem=ar_s.at[k],
                recv_sem=ar_r.at[stage, there], device_id=mate, device_id_type=MESH,
            ).wait_recv()
        total = ar[stage, 0] + ar[stage, 1]
        for k in range(2, count):
            total += ar[stage, k]
        small[...] = total

    loads["wout"].wait()
    weight_begin()
    loads["tok"].wait()
    loads["win"].wait()
    mixer_in(0)
    pl.semaphore_wait(barrier, len(partners))
    weight_far()
    mixer_out(0)
    mixer_in(1)
    send_halo()
    mixer_out(1)
    weight_first()
    loads["cot"].wait()
    loads["wd"].wait()
    grad_hidden(0)
    grad_hidden(1)
    weight_second()
    mixer_edge()
    mix_pass(0)
    weight_near()
    for k in range(3):
        mix_near(k)
    branch(h, tok)
    mix_pass(1)
    weight_third()
    mix_pass(2)
    loads["wg"].wait()
    loads["wu"].wait()
    for k in range(3):
        mix_end(k)
    weight_end()
    branch(1 - h, mid)
    ffn_norm()
    for tile in TILES[:2]:
        ffn_tiles([tile])
        product_down([tile])
    ring_begin(0, (0, 512))
    ffn_tiles(TILES[2:])
    product_down(TILES[2:])
    ring_begin(0, (512, 640))
    ring_fill(0)
    ffn_back(0)
    ffn_back(1)
    sum_cross(1, 0)
    sum_cross(1, 1)
    product(1, aff, gg[...], 0, HID)
    ring_relay(0)
    ring_begin(1)
    ring_fill(1)
    sum_share(1, 0)
    sum_end(1, 0)
    mixer_back(0)
    ring_turn(0)
    ring_sent(0, first)
    product(0, aff, gu[...], 0, HID)
    ffn_out(0)
    sum_cross(3, 0)
    ring_relay(1)
    ring_begin(2)
    sum_share(1, 1)
    sum_end(1, 1)
    mixer_back(1)
    product_out()
    pair_begin()
    mixer_back_in(0)
    ring_fill(2)
    ffn_out(1)
    sum_cross(2, 0)
    ring_relay_two(0)
    mixer_back_in(1)
    ring_turn(1)
    ring_sent(1, first)
    sum_cross(2, 1)
    for g in (0, 1):
        aff[rows_of(g)] = normed(g)
    product(1, aff, gg[:, 0 : 3 * CH], 0, 3 * CH)
    ring_begin(3)
    ring_relay(2)
    pair_end()
    ring_begin(4)
    ring_cross(0)
    sum_share(3, 0)
    sum_end(3, 0)
    result_out(0)
    result_out(1)
    ring_relay_two(1)
    ring_fill(3)
    ring_fill(4)
    sum_share(2, 0)
    sum_cross(3, 1)
    ring_sent(0, second)
    ring_relay(3)
    sum_end(2, 0)
    for r in (0, 1):
        tokens_out(r)
    ring_turn(2)
    ring_relay(4)
    sum_share(2, 1)
    sum_end(2, 1)
    for r in (2, 3):
        tokens_out(r)
    small_begin(0)
    ring_cross(1)
    ring_sent(1, second)
    ring_turn(3)
    ring_relay_two(2)
    ring_turn(4)
    small_end(0)
    small_begin(1)
    sum_share(3, 1)
    ring_cross(3)
    ring_end(0)
    ring_end(1)
    small_end(1)
    small_begin(2)
    ring_cross(2)
    ring_cross(4)
    sum_end(3, 1)
    for r in (2, 3):
        result_out(r)
    small_end(2)
    leave(small, o_small)
    for job in range(2, 5):
        ring_sent(job, first)
        ring_sent(job, second)
    ring_end(3)
    ring_end(2)
    for copy in outs:
        copy.wait()


def finish(*refs):
    ins, outs, held, sem = refs[:8], refs[8:18], refs[18:28], refs[28]
    parts = [(k, r) for r in range(ROWS) for k in range(2)] + [(k, None) for k in range(2, 10)]

    def move(way, n):
        k, r = parts[n]
        src, dst = ((ins, held), (held, outs))[way]
        if r is None:
            return pltpu.make_async_copy(src[k], dst[k], sem.at[way, n])
        return pltpu.make_async_copy(src[k].at[r], dst[k].at[r], sem.at[way, n])

    incoming = [move(0, n) for n in range(13)]
    for copy in incoming:
        copy.start()
    small = ins[7]
    held[7][...] = small[1]
    held[8][...] = small[0]
    held[9][...] = small[2:5, 0:CH]
    outgoing = [move(1, n) for n in range(13, 16)]
    for copy in outgoing:
        copy.start()
    for n, copy in enumerate(incoming):
        copy.wait()
        outgoing.append(move(1, n))
        outgoing[-1].start()
    for copy in outgoing:
        copy.wait()


def on_device(
    tokens, start_flags, norm_one, w_in, w_conv, w_out, norm_two, w_gate, w_up, w_down, cotangent
):
    any_spec = pl.BlockSpec(memory_space=pl.ANY)
    vmem = pl.BlockSpec(memory_space=pltpu.VMEM)
    dma = pltpu.SemaphoreType.DMA
    shape = jax.ShapeDtypeStruct
    outs = pl.pallas_call(
        kernel,
        out_shape=(
            shape((ROWS, TB, D), F32),
            shape((ROWS, TB, D), F32),
            shape((3, 32, CH), F32),
            shape((32, CH), F32),
            shape((32, HID), F32),
            shape((32, HID), F32),
            shape((32, HID), F32),
            shape((8, D), F32),
        ),
        in_specs=[pl.BlockSpec(memory_space=pltpu.SMEM)] + [any_spec] * 7 + [vmem] * 3,
        out_specs=(any_spec,) * 8,
        scratch_shapes=[
            pltpu.VMEM((ROWS, TB, D), F32),
            pltpu.VMEM((ROWS, TB, D), F32),
            pltpu.VMEM((3, D, CH), BF16),
            pltpu.VMEM((D, CH), BF16),
            pltpu.VMEM((D, HID), BF16),
            pltpu.VMEM((D, HID), BF16),
            pltpu.VMEM((D, HID), BF16),
            pltpu.VMEM((3, POS, CH), F32),
            pltpu.VMEM((ROWS, TB + 8, CH), F32),
            pltpu.VMEM((ROWS, TB + 8, CH), F32),
            pltpu.VMEM((ROWS, TB, D), F32),
            pltpu.VMEM((POS, D), BF16),
            pltpu.VMEM((POS, HID), BF16),
            pltpu.VMEM((POS, HID), BF16),
            pltpu.VMEM((POS, HID), BF16),
            pltpu.VMEM((2, POS, POS), BF16),
            pltpu.VMEM((POS, HID), F32),
                pltpu.VMEM((ROWS, 8, CH), F32),
            pltpu.VMEM((ROWS, 8, CH), F32),
            pltpu.VMEM((ROWS, 8, CH), F32),
            pltpu.VMEM((2, ROWS, TB, D), F32),
            pltpu.VMEM((2, ROWS, HALF, D), F32),
            pltpu.VMEM((3, ROWS, HALF, D), F32),
            pltpu.VMEM((2, ROWS, HALF, D), F32),
            pltpu.VMEM((2, 4, 4, 2, 32, HID), F32),
            pltpu.VMEM((2, 2, 2, 2, 32, HID), F32),
            pltpu.VMEM((2, 2, 2, 4, 32, HID), F32),
            pltpu.VMEM((4, 2, 2, 16, HID), F32),
            pltpu.VMEM((4, 2, 2, 32, HID), F32),
            pltpu.VMEM((4, 32, HID), F32),
            pltpu.VMEM((4, 4, 2, 32, CH), F32),
            pltpu.VMEM((4, 4, 32, CH), F32),
            pltpu.VMEM((8, D), F32),
            pltpu.VMEM((3, 4, 8, D), F32),
            dma((7,)),
            dma((16,)),
            dma((3, 3)),
            dma((3, 3)),
            dma((22,)),
            dma((22,)),
            dma((3,)),
            dma((3,)),
            dma((2, 2)),
            dma((3, 2)),
            dma((2, 2)),
            dma((3, 2)),
            dma((2, 2)),
            dma((3, 2)),
            dma((3, 2, 6)),
            dma((3, 2, 6)),
            dma((2, 4)),
            dma((2, 4)),
            dma((3, 2, 6)),
            dma((5, 2, 6)),
            dma((4,)),
            dma((4,)),
            dma((1,)),
            dma((1,)),
            dma((3,)),
            dma((3, 4)),
            pltpu.SemaphoreType.REGULAR((2, 2, 2)),
        ],
        compiler_params=pltpu.CompilerParams(
            collective_id=0, has_side_effects=True, vmem_limit_bytes=63 * 2**20
        ),
        name="block",
    )(
        start_flags.T, tokens, cotangent, w_in, w_out, w_gate, w_up, w_down,
        norm_one.reshape(1, D), norm_two.reshape(1, D), w_conv,
    )
    result, grad_tokens, g_in, g_out, g_gate, g_up, g_down, one, two, taps = pl.pallas_call(
        finish,
        out_shape=tuple(shape(o.shape, F32) for o in outs[:2])
        + (
            shape((3, 32, CH), F32),
            shape((32, CH), F32),
            shape((32, HID), F32),
            shape((32, HID), F32),
            shape((32, HID), F32),
            shape((D,), F32),
            shape((D,), F32),
            shape((3, CH), F32),
        ),
        in_specs=[any_spec] * 7 + [vmem],
        out_specs=(any_spec,) * 10,
        scratch_shapes=[pltpu.VMEM(o.shape, F32) for o in outs[:7]]
        + [pltpu.VMEM(d, F32) for d in ((D,), (D,), (3, CH))]
        + [dma((2, 16))],
        compiler_params=pltpu.CompilerParams(vmem_limit_bytes=60 * 2**20),
        name="finish",
    )(*outs)
    return result, grad_tokens, one, g_in, taps, g_out, two, g_gate, g_up, g_down


def solution(mesh):
    return jax.shard_map(
        on_device,
        mesh=mesh,
        in_specs=(
            P(None, "seq", None),
            P(None, "seq"),
            P(),
            P(None, None, "wt"),
            P(None, "wt"),
            P(None, "wt"),
            P(),
            P(None, "wt"),
            P(None, "wt"),
            P(None, "wt"),
            P(None, "seq", None),
        ),
        out_specs=(
            P(None, "seq", None),
            P(None, "seq", None),
            P(),
            P(None, "seq", "wt"),
            P(None, "wt"),
            P("seq", "wt"),
            P(),
            P("seq", "wt"),
            P("seq", "wt"),
            P("seq", "wt"),
        ),
        check_vma=False,
    )
```

```python
import functools

import jax
import jax.numpy as jnp
from jax import lax
from jax.experimental import pallas as pl
from jax.experimental.pallas import tpu as pltpu
from jax.sharding import PartitionSpec as P

EPS = 1e-05
MESH = pl.DeviceIdType.MESH
F32 = jnp.float32
BF16 = jnp.bfloat16
NN = ((1,), (0,))
NT = ((1,), (1,))
TN = ((0,), (0,))

ROWS, TB, D, CH, HID = 4, 128, 1024, 256, 1152
POS = ROWS * TB
HALF = TB // 2
JOBS = (
    (0, 0, HID, 32),
    (1, 0, HID, 32),
    (0, 0, HID, 32),
    (1, 0, 3 * CH, 32),
    (1, 3 * CH, CH, 16),
)
TILES = ((0, 256), (256, 256), (512, 256), (768, 256), (1024, 128))


def mm(a, b, dims):
    return lax.dot_general(a, b, (dims, ((), ())), preferred_element_type=F32)


def kernel(
    flags, tokens, cotangent, w_in, w_out, w_gate, w_up, w_down, norm_one, norm_two, w_conv,
    result, grad_tokens, o_in, o_out, o_gate, o_up, o_down, o_small,
    tok, cot, win, wout, wg, wu, wd,
    proj, bxe, gce, mid, aff, hid, gg, gu, gf, gh, sbuf, hf, hb,
    part, c_recv, x_recv, a_recv,
    grads, rel1, fin1, rel2, fin2, last, grads_out, paired, small, ar,
    in_sem, out_sem, m_s, m_r, v_s, v_r, h_s, h_r, c_s, c_r, x_s, x_r, a_s, a_r,
    s1_s, s1_r, split_s, split_r, s2_s, s2_r, s3_s, s3_r, p_s, p_r, ar_s, ar_r, credit,
):
    s = lax.axis_index("seq")
    w = lax.axis_index("wt")
    y, z, l = s // 8, (s // 2) % 4, s % 2
    h, c = w // 2, w % 2

    def dev(y=y, z=z, l=l, h=h, c=c):
        return ((y * 4 + z) * 2 + l, h * 2 + c)

    def up(v, by=1):
        return (v + by) % 4

    plus = (dev(y=up(y)), dev(z=up(z)))
    minus = (dev(y=up(y, 3)), dev(z=up(z, 3)))
    across = dev(l=1 - l)
    far = dev(h=1 - h)
    mate = dev(c=1 - c)
    following = ((s + 1) % 32, w)
    previous = ((s + 31) % 32, w)

    def remote(src, dst, send, recv, to):
        copy = pltpu.make_async_remote_copy(
            src_ref=src, dst_ref=dst, send_sem=send, recv_sem=recv, device_id=to, device_id_type=MESH
        )
        copy.start()
        return copy

    loads = {}

    def load(name, src, dst):
        loads[name] = pltpu.make_async_copy(src, dst, in_sem.at[len(loads)])
        loads[name].start()

    load("wout", w_out, wout)
    load("tok", tokens, tok)
    load("win", w_in, win)
    load("cot", cotangent, cot)
    load("wd", w_down, wd)
    load("wg", w_gate, wg)
    load("wu", w_up, wu)

    barrier = pltpu.get_barrier_semaphore()
    partners = (
        plus + minus + (dev(y=up(y, 2)), dev(z=up(z, 2)), across, far, mate, following, previous)
    )
    for partner in partners:
        pl.semaphore_signal(barrier, inc=1, device_id=partner, device_id_type=MESH)

    small[...] = jnp.zeros_like(small)

    def rows_of(g):
        return pl.ds(g * 2 * TB, 2 * TB)

    keep = [1.0 - (flags[0, r] == 1).astype(F32) for r in range(ROWS)]

    halo = {}

    def normed(g):
        t = tok[2 * g : 2 * g + 2].reshape(2 * TB, D)
        scale = lax.rsqrt(jnp.mean(t * t, axis=-1, keepdims=True) + EPS)
        return (t * scale * norm_one[...]).astype(BF16)

    def mixer_in(g):
        act = normed(g)
        for j in range(3):
            proj[j, rows_of(g)] = mm(act, win[j], NN)
        bx = proj[0, rows_of(g)] * proj[2, rows_of(g)]
        for k in range(2):
            bxe[2 * g + k, 8:] = bx[k * TB : (k + 1) * TB]

    def send_halo():
        halo[0] = remote(bxe.at[:, pl.ds(TB, 8)], hf, h_s.at[2], h_r.at[2], following)

    mine = pl.ds(pl.multiple_of(w * CH, CH), CH)
    theirs = pl.ds(pl.multiple_of(((1 - h) * 2 + c) * CH, CH), CH)
    weight = {}

    def weight_begin():
        @pl.loop(0, 4)
        def _(i):
            rows = pl.ds(pl.multiple_of(i * 256, 256), 256)
            grads[1, i, :, :, :, mine] = wout[rows].astype(F32).reshape(4, 2, 32, CH)

    def weight_far():
        block = grads.at[1, y, z, :, :, mine]
        weight["far"] = remote(block, block, v_s.at[0], v_r.at[0], far)
        block = grads.at[1, :, :, :, :, mine]
        weight["mate"] = remote(block, block, v_s.at[1], v_r.at[1], mate)

    def weight_first():
        weight["far"].wait_recv()
        for p in range(2):
            for k in (1, 2, 3):
                to = dev(y=up(y, k)) if p == 0 else dev(z=up(z, k))
                block = grads.at[1, y, z, p, :, theirs]
                weight["first", p, k] = remote(
                    block, block, v_s.at[1 + p * 3 + k], v_r.at[1 + p * 3 + k], to
                )

    def weight_row(p, j):
        return grads.at[1, :, j, 0, :, theirs] if p == 0 else grads.at[1, j, :, 1, :, theirs]

    def weight_pass(p, k):
        block = weight_row(p, up((z, y)[p], 4 - k))
        weight["pass", p, k] = remote(
            block, block, v_s.at[14 + p * 4 + k], v_r.at[14 + p * 4 + k], mate
        )

    def weight_second():
        for p in range(2):
            for k in (1, 2, 3):
                weight["first", p, k].wait_recv()
        for p in range(2):
            for k in (1, 2, 3):
                to = dev(z=up(z, k)) if p == 0 else dev(y=up(y, k))
                block = weight_row(p, (z, y)[p])
                weight["second", p, k] = remote(
                    block, block, v_s.at[7 + p * 3 + k], v_r.at[7 + p * 3 + k], to
                )
        for p in range(2):
            weight_pass(p, 0)

    def weight_third():
        for k in (1, 3, 2):
            for p in range(2):
                weight["second", p, k].wait_recv()
                weight_pass(p, k)

    def weight_near():
        weight["mate"].wait()

    def weight_end():
        weight["far"].wait_send()
        for p in range(2):
            for k in (1, 2, 3):
                weight["first", p, k].wait_send()
                weight["second", p, k].wait_send()
            for k in range(4):
                weight["pass", p, k].wait()

    mix = {}

    def mix_block(k, columns):
        if k < 2:
            return part.at[0, pl.ds(2 * k, 2), pl.ds(8, TB - 8), columns]
        return part.at[0, :, pl.ds(0, 8), columns]

    def mix_send(k):
        block = mix_block(k, mine)
        mix["far", k] = remote(block, block, m_s.at[0, k], m_r.at[0, k], far)
        mix["mate", k] = remote(block, block, m_s.at[1, k], m_r.at[1, k], mate)

    def mix_pass(k):
        mix["far", k].wait_recv()
        block = mix_block(k, theirs)
        mix["pass", k] = remote(block, block, m_s.at[2, k], m_r.at[2, k], mate)

    def mix_near(k):
        mix["mate", k].wait()

    def mix_end(k):
        mix["far", k].wait_send()
        mix["pass", k].wait()

    def conv(r, at, count):
        return (
            w_conv[0:1] * bxe[r, at + 6 : at + 6 + count]
            + w_conv[1:2] * bxe[r, at + 7 : at + 7 + count]
            + w_conv[2:3] * bxe[r, at + 8 : at + 8 + count]
        )

    def taps(r, at, count):
        total = conv(r, at, count)
        rows = pl.ds(r * TB + at, count)
        part[0, r, at : at + count, mine] = (proj[1, rows] * total).astype(BF16).astype(F32)

    def mixer_out(g):
        for r in (2 * g, 2 * g + 1):
            taps(r, 8, TB - 8)
        mix_send(g)

    def mixer_edge():
        halo[0].wait()
        for r in range(4):
            bxe[r, 0:8] = hf[r] * keep[r]
            taps(r, 0, 8)
        mix_send(2)

    def branch(chip, start):
        half = pl.ds(pl.multiple_of(chip * 2 * CH, 2 * CH), 2 * CH)
        left = part[0, :, :, half].reshape(POS, 2 * CH).astype(BF16)
        for i in range(4):
            right = grads[1, i, :, :, :, half].reshape(256, 2 * CH).astype(BF16)
            columns = pl.ds(i * 256, 256)
            mid[:, :, columns] = start[:, :, columns] + mm(left, right, NT).reshape(ROWS, TB, 256)

    csend, xsend, asend = {}, {}, {}
    own = pl.ds(pl.multiple_of(c * HALF, HALF), HALF)
    other = pl.ds(pl.multiple_of((1 - c) * HALF, HALF), HALF)
    bank_of = (None, 1, 0, 1)

    def sum_begin(q, g):
        b, two = bank_of[q], pl.ds(2 * g, 2)
        csend[q, g] = remote(part.at[b, two, other], c_recv.at[b, two], c_s.at[b, g], c_r.at[q - 1, g], mate)

    def sum_cross(q, g):
        b, two = bank_of[q], pl.ds(2 * g, 2)
        csend[q, g].wait_recv()
        part[b, two, own] = part[b, two, own] + c_recv[b, two]
        xsend[q, g] = remote(part.at[b, two, own], x_recv.at[q - 1, two], x_s.at[b, g], x_r.at[q - 1, g], far)

    def sum_share(q, g):
        b, two = bank_of[q], pl.ds(2 * g, 2)
        xsend[q, g].wait()
        part[b, two, own] = part[b, two, own] + x_recv[q - 1, two]
        asend[q, g] = remote(part.at[b, two, own], a_recv.at[b, two], a_s.at[b, g], a_r.at[q - 1, g], mate)

    def sum_end(q, g):
        b, two = bank_of[q], pl.ds(2 * g, 2)
        csend[q, g].wait_send()
        asend[q, g].wait()
        part[b, two, other] = a_recv[b, two]

    def grad_hidden(g):
        whole = cot[2 * g : 2 * g + 2].reshape(2 * TB, D)
        value = whole.astype(BF16)
        for i in range(2):
            gf[i, :, g * 256 : (g + 1) * 256] = whole[:, i * POS : (i + 1) * POS].T.astype(BF16)
        for n, width in TILES:
            gh[rows_of(g), n : n + width] = mm(value, wd[:, n : n + width], NN)

    def ffn_norm():
        for r in range(ROWS):
            m = mid[r]
            scale = lax.rsqrt(jnp.mean(m * m, axis=-1, keepdims=True) + EPS)
            aff[r * TB : (r + 1) * TB] = (m * scale * norm_two[...]).astype(BF16)

    def ffn_tiles(tiles):
        act = aff[...]
        for n, width in tiles:
            at = (slice(None), slice(n, n + width))
            gate = mm(act, wg[at], NN)
            upv = mm(act, wu[at], NN)
            sig = jax.nn.sigmoid(gate)
            silu = gate * sig
            grad = gh[at]
            hid[at] = (silu * upv).astype(BF16)
            gu[at] = (grad * silu).astype(BF16)
            gg[at] = (grad * upv * sig * (1.0 + gate * (1.0 - sig))).astype(BF16)

    def ffn_back(g):
        partial = mm(gg[rows_of(g)], wg[...], NT) + mm(gu[rows_of(g)], wu[...], NT)
        part[1, 2 * g : 2 * g + 2] = partial.reshape(2, TB, D)
        sum_begin(1, g)

    def ffn_out(g):
        partial = mm(hid[rows_of(g)], wd[...], NT)
        part[1, 2 * g : 2 * g + 2] = partial.reshape(2, TB, D)
        sum_begin(3, g)

    def product(slot, left, right, n, width):
        @pl.loop(0, 4)
        def _(i):
            columns = pl.ds(pl.multiple_of(i * 256, 256), 256)
            value = mm(left[:, columns], right, TN)
            value = value.reshape(4, 2, 32, width)
            grads[slot, i, :, :, :, n : n + width] = value

    def product_down(tiles):
        for n, width in tiles:
            right = hid[:, n : n + width]
            for i in range(2):
                value = mm(gf[i], right, NN).reshape(2, 4, 2, 32, width)
                grads[0, 2 * i : 2 * i + 2, :, :, :, n : n + width] = value

    def product_out():
        right = wg[0:POS, 0:CH]
        for i in range(4):
            left = gf[i // 2, :, i % 2 * 256 : (i % 2 + 1) * 256]
            grads_out[i] = mm(left, right, TN).reshape(4, 2, 32, CH)

    outs = []

    def leave(src, dst):
        outs.append(pltpu.make_async_copy(src, dst, out_sem.at[len(outs)]))
        outs[-1].start()

    place = (y, z)

    def slot_of(job):
        return 2 if job == 4 else job % 2

    def block_of(job):
        slot, at, n, deep = JOBS[job]
        return slot, pl.ds(at, n), pl.ds(0, deep), deep

    def sems_of(job, p, k):
        if k >= 6:
            return split_s.at[p, k - 6], split_r.at[p, k - 6]
        return s1_s.at[slot_of(job), p, k], s1_r.at[slot_of(job), p, k]

    def chunk(job, p, j, half=None, columns=None):
        slot, every, rows, deep = block_of(job)
        columns = every if columns is None else columns
        cut = pl.ds(0, 4) if half is None else pl.ds(2 * half, 2)
        if deep != 32:
            rows = pl.ds(deep * p, deep)
            return grads_out.at[j, cut, l, rows] if p == 0 else grads_out.at[cut, j, l, rows]
        if p == 0:
            return grads.at[slot, j, cut, 0, rows, columns]
        return grads.at[slot, cut, j, 1, rows, columns]

    pair = []

    def pair_begin():
        pair.append(remote(grads_out.at[:, :, 1 - l], paired, p_s.at[0], p_r.at[0], across))

    def pair_end():
        pair[0].wait()

        @pl.loop(0, 4)
        def _(i):
            grads_out[i, :, l] = grads_out[i, :, l] + paired[i]

    first = {}

    def ring_begin(job, cut=None):
        slot, columns, rows, _ = block_of(job)
        columns, base = (columns, 0) if cut is None else (pl.ds(*cut), 6 if cut[0] else 0)
        for p in range(2):
            i = place[p]
            if job in (2, 3):
                pl.semaphore_wait(credit.at[slot, p, 0], 1)
                pl.semaphore_wait(credit.at[slot, p, 1], 1)
            copies = first.setdefault((job, p), {})
            for k, half, to in ((0, 0, plus[p]), (1, 1, minus[p])):
                copies[base + k] = remote(
                    chunk(job, p, up(i, 2), half, columns), rel1.at[slot, p, k, :, rows, columns],
                    *sems_of(job, p, base + k), to,
                )

    def ring_fill(job, cut=None):
        slot, columns, rows, _ = block_of(job)
        columns, base = (columns, 2) if cut is None else (pl.ds(*cut), 8 if cut[0] else 2)
        for p in range(2):
            i = place[p]
            for k, half, to in ((0, 1, plus[p]), (1, 0, minus[p])):
                first[job, p][base + k] = remote(
                    chunk(job, p, up(i, 1 + 2 * k), half, columns),
                    fin1.at[slot, p, k, pl.ds(2 * half, 2), rows, columns],
                    *sems_of(job, p, base + k), to,
                )

    def ring_relay(job):
        slot, columns, rows, _ = block_of(job)
        for p in range(2):
            i = place[p]
            copies = first[job, p]
            for k, j, half, to in ((0, up(i), 0, plus[p]), (1, up(i, 3), 1, minus[p])):
                copies[k].wait_recv()
                if 6 + k in copies:
                    copies[6 + k].wait_recv()
                target = chunk(job, p, j, half)
                for m in range(2):
                    target[m] = target[m] + rel1[slot, p, k, m, rows, columns]
                copies[4 + k] = remote(
                    target, fin1.at[slot, p, k, pl.ds(2 * half, 2), rows, columns],
                    s1_s.at[slot_of(job), p, 4 + k], s1_r.at[slot_of(job), p, 4 + k], to,
                )

    second = {}

    def piece(job, p, j, half=None):
        slot, columns, _, deep = block_of(job)
        row = (slot * 2 + p) * 128 + j * 32
        if half is None:
            return gh.at[pl.ds(pl.multiple_of(row, 32), deep), columns]
        return gh.at[pl.ds(pl.multiple_of(row + deep // 2 * half, 8), deep // 2), columns]

    def ring_turn(job):
        slot, columns, rows, deep = block_of(job)
        at, cut = min(job, 3), (pl.ds(0, deep // 2), pl.ds(deep // 2, deep // 2))
        for p in range(2):
            for k in (2, 3, 8, 9, 4, 5):
                if k in first[job, p]:
                    first[job, p][k].wait_recv()
            mine = chunk(job, p, place[p])

            @pl.loop(0, 4)
            def _(m):
                to = pl.ds(pl.multiple_of((slot * 2 + p) * 128 + m * 32, 32), deep)
                gh[to, columns] = (
                    mine[m] + fin1[slot, p, 0, m, rows, columns] + fin1[slot, p, 1, m, rows, columns]
                )

            if job < 2:
                pl.semaphore_signal(credit.at[slot, p, 0], inc=1, device_id=minus[p], device_id_type=MESH)
                pl.semaphore_signal(credit.at[slot, p, 1], inc=1, device_id=plus[p], device_id_type=MESH)
            i = place[1 - p]
            sems = lambda k: (s2_s.at[slot_of(job), p, k], s2_r.at[job, p, k])
            a, b = plus[1 - p], minus[1 - p]
            if job >= 3:
                beyond = dev(z=up(z, 2)) if p == 0 else dev(y=up(y, 2))
                second[job, p] = {
                    0: remote(piece(job, p, up(i, 2), 0), rel2.at[at, p, 0, cut[0], columns], *sems(0), beyond),
                    1: remote(piece(job, p, up(i, 2), 1), rel2.at[at, p, 1, cut[0], columns], *sems(1), beyond),
                    2: remote(piece(job, p, up(i)), fin2.at[at, p, 0, rows, columns], *sems(2), a),
                    3: remote(piece(job, p, up(i, 3)), fin2.at[at, p, 1, rows, columns], *sems(3), b),
                }
                continue
            second[job, p] = {
                0: remote(piece(job, p, up(i, 2), 0), rel2.at[at, p, 0, cut[0], columns], *sems(0), a),
                1: remote(piece(job, p, up(i, 2), 1), rel2.at[at, p, 1, cut[0], columns], *sems(1), b),
                2: remote(piece(job, p, up(i), 1), fin2.at[at, p, 0, cut[1], columns], *sems(2), a),
                3: remote(piece(job, p, up(i, 3), 0), fin2.at[at, p, 1, cut[0], columns], *sems(3), b),
            }

    def ring_relay_two(job):
        _, columns, _, deep = block_of(job)
        at, cut = min(job, 3), (pl.ds(0, deep // 2), pl.ds(deep // 2, deep // 2))
        for p in range(2):
            i = place[1 - p]
            copies = second[job, p]
            for k, j, half, to in ((0, up(i), 0, plus[1 - p]), (1, up(i, 3), 1, minus[1 - p])):
                copies[k].wait_recv()
                target = piece(job, p, j, half)
                target[...] = target[...] + rel2[at, p, k, cut[0], columns]
                copies[4 + k] = remote(
                    target, fin2.at[at, p, k, cut[half], columns],
                    s2_s.at[slot_of(job), p, 4 + k], s2_r.at[job, p, 4 + k], to,
                )

    third = {}

    def ring_cross(job):
        _, columns, rows, deep = block_of(job)
        at = min(job, 3)
        for p in range(2):
            for k in (2, 3, 0, 1) if job >= 3 else (2, 3, 4, 5):
                second[job, p][k].wait_recv()
            total = (
                piece(job, p, place[1 - p])[...]
                + fin2[at, p, 0, rows, columns]
                + fin2[at, p, 1, rows, columns]
            )
            if job >= 3:
                low = pl.ds(0, deep // 2)
                total += jnp.concatenate([rel2[at, p, 0, low, columns], rel2[at, p, 1, low, columns]], axis=0)
            if deep == 32:
                fin2[at, p, 0, :, columns] = total
            else:
                paired[0, 0, p * deep : (p + 1) * deep] = total
        if deep != 32:
            leave(paired.at[0, 0], o_out)
        else:
            third[job] = remote(
                fin2.at[at, 1 - l, 0, :, columns], last.at[at, :, columns], s3_s.at[job], s3_r.at[job], across
            )

    def ring_end(job):
        columns = block_of(job)[1]
        third[job].wait()
        last[job, :, columns] = fin2[job, l, 0, :, columns] + last[job, :, columns]
        if job < 3:
            leave(last.at[job], (o_down, o_gate, o_up)[job])
        else:
            for j in range(3):
                leave(last.at[job, :, pl.ds(j * CH, CH)], o_in.at[j])

    def ring_sent(job, copies):
        for p in range(2):
            for copy in copies[job, p].values():
                copy.wait_send()

    back = {}

    def mixer_back(g):
        for r in (2 * g, 2 * g + 1):
            rows = pl.ds(r * TB, TB)
            m, grad = mid[r], part[1, r]
            scale = lax.rsqrt(jnp.mean(m * m, axis=-1, keepdims=True) + EPS)
            small[0:1] += jnp.sum(grad * m * scale, axis=0, keepdims=True)
            weighted = grad * norm_two[...]
            total = (
                cot[r]
                + scale * weighted
                - m * (scale * scale * scale) * jnp.mean(weighted * m, axis=-1, keepdims=True)
            )
            cot[r] = total
            for i in range(2):
                gf[i, rows] = total[:, i * POS : (i + 1) * POS].astype(BF16)
        gmix = mm(gf[0, rows_of(g)], wout[0:POS], NN) + mm(gf[1, rows_of(g)], wout[POS:], NN)
        for k in range(2):
            r = 2 * g + k
            rows = pl.ds(r * TB, TB)
            value = gmix[k * TB : (k + 1) * TB]
            total = conv(r, 0, TB)
            gg[rows, CH : 2 * CH] = (value * total).astype(BF16)
            wg[rows, 0:CH] = (proj[1, rows] * total).astype(BF16)
            gce[r, 0:TB] = value * proj[1, rows]
            sbuf[r] = gce[r, 0:8] * keep[r]
        two = pl.ds(2 * g, 2)
        back[g] = remote(sbuf.at[two], hb.at[two], h_s.at[g], h_r.at[g], previous)

    def mixer_back_in(g):
        back[g].wait()
        for r in (2 * g, 2 * g + 1):
            rows = pl.ds(r * TB, TB)
            gce[r, TB:] = hb[r]
            value = gce[r, 0:TB]
            for k in range(3):
                small[2 + k : 3 + k, 0:CH] += jnp.sum(
                    value * bxe[r, 6 + k : 6 + k + TB], axis=0, keepdims=True
                )
            gbx = w_conv[2:3] * value + w_conv[1:2] * gce[r, 1 : 1 + TB] + w_conv[0:1] * gce[r, 2 : 2 + TB]
            gg[rows, 0:CH] = (gbx * proj[2, rows]).astype(BF16)
            gg[rows, 2 * CH : 3 * CH] = (gbx * proj[0, rows]).astype(BF16)
        partial = mm(gg[rows_of(g), 0:CH], win[0], NT)
        for j in (1, 2):
            partial += mm(gg[rows_of(g), j * CH : (j + 1) * CH], win[j], NT)
        part[0, 2 * g : 2 * g + 2] = partial.reshape(2, TB, D)
        sum_begin(2, g)

    def tokens_out(r):
        t, grad = tok[r], part[0, r]
        scale = lax.rsqrt(jnp.mean(t * t, axis=-1, keepdims=True) + EPS)
        small[1:2] += jnp.sum(grad * t * scale, axis=0, keepdims=True)
        weighted = grad * norm_one[...]
        cot[r] = (
            cot[r]
            + scale * weighted
            - t * (scale * scale * scale) * jnp.mean(weighted * t, axis=-1, keepdims=True)
        )
        leave(cot.at[r], grad_tokens.at[r])

    def result_out(r):
        mid[r] = mid[r] + part[1, r]
        leave(mid.at[r], result.at[r])

    reduced = {}

    def small_begin(stage):
        at, peers = (
            (l, [across]),
            (y, [dev(y=up(y, k)) for k in (1, 2, 3)]),
            (z, [dev(z=up(z, k)) for k in (1, 2, 3)]),
        )[stage]
        ar[stage, at] = small[...]
        reduced[stage] = [
            remote(small, ar.at[stage, at], ar_s.at[k], ar_r.at[stage, at], to)
            for k, to in enumerate(peers)
        ]

    def small_end(stage):
        at, count = ((l, 2), (y, 4), (z, 4))[stage]
        for k, copy in enumerate(reduced[stage]):
            copy.wait_send()
            there = (at + k + 1) % count
            pltpu.make_async_remote_copy(
                src_ref=small, dst_ref=ar.at[stage, there], send_sem=ar_s.at[k],
                recv_sem=ar_r.at[stage, there], device_id=mate, device_id_type=MESH,
            ).wait_recv()
        total = ar[stage, 0] + ar[stage, 1]
        for k in range(2, count):
            total += ar[stage, k]
        small[...] = total

    loads["wout"].wait()
    weight_begin()
    loads["tok"].wait()
    loads["win"].wait()
    mixer_in(0)
    pl.semaphore_wait(barrier, len(partners))
    weight_far()
    mixer_out(0)
    mixer_in(1)
    send_halo()
    mixer_out(1)
    weight_first()
    loads["cot"].wait()
    loads["wd"].wait()
    grad_hidden(0)
    grad_hidden(1)
    weight_second()
    mixer_edge()
    mix_pass(0)
    weight_near()
    for k in range(3):
        mix_near(k)
    branch(h, tok)
    mix_pass(1)
    weight_third()
    mix_pass(2)
    loads["wg"].wait()
    loads["wu"].wait()
    for k in range(3):
        mix_end(k)
    weight_end()
    branch(1 - h, mid)
    ffn_norm()
    for tile in TILES[:2]:
        ffn_tiles([tile])
        product_down([tile])
    ring_begin(0, (0, 512))
    ffn_tiles(TILES[2:])
    product_down(TILES[2:])
    ring_begin(0, (512, 640))
    ring_fill(0)
    ffn_back(0)
    ffn_back(1)
    sum_cross(1, 0)
    sum_cross(1, 1)
    product(1, aff, gg[...], 0, HID)
    ring_relay(0)
    ring_begin(1)
    ring_fill(1)
    sum_share(1, 0)
    sum_end(1, 0)
    mixer_back(0)
    ring_turn(0)
    ring_sent(0, first)
    product(0, aff, gu[...], 0, HID)
    ffn_out(0)
    sum_cross(3, 0)
    ring_relay(1)
    ring_begin(2)
    sum_share(1, 1)
    sum_end(1, 1)
    mixer_back(1)
    product_out()
    pair_begin()
    mixer_back_in(0)
    ring_fill(2)
    ffn_out(1)
    sum_cross(2, 0)
    ring_relay_two(0)
    mixer_back_in(1)
    ring_turn(1)
    ring_sent(1, first)
    sum_cross(2, 1)
    for g in (0, 1):
        aff[rows_of(g)] = normed(g)
    product(1, aff, gg[:, 0 : 3 * CH], 0, 3 * CH)
    ring_begin(3)
    ring_relay(2)
    pair_end()
    ring_begin(4)
    ring_cross(0)
    sum_share(3, 0)
    sum_end(3, 0)
    result_out(0)
    result_out(1)
    ring_relay_two(1)
    ring_fill(3)
    ring_fill(4)
    sum_share(2, 0)
    ring_sent(0, second)
    ring_relay(3)
    sum_end(2, 0)
    for r in (0, 1):
        tokens_out(r)
    ring_turn(2)
    ring_relay(4)
    sum_share(2, 1)
    sum_end(2, 1)
    for r in (2, 3):
        tokens_out(r)
    small_begin(0)
    sum_cross(3, 1)
    ring_cross(1)
    ring_sent(1, second)
    ring_turn(3)
    small_end(0)
    small_begin(1)
    ring_relay_two(2)
    ring_turn(4)
    ring_cross(3)
    small_end(1)
    small_begin(2)
    ring_end(0)
    ring_end(1)
    sum_share(3, 1)
    ring_cross(2)
    ring_cross(4)
    sum_end(3, 1)
    for r in (2, 3):
        result_out(r)
    small_end(2)
    leave(small, o_small)
    for job in range(2, 5):
        ring_sent(job, first)
        ring_sent(job, second)
    ring_end(3)
    ring_end(2)
    for copy in outs:
        copy.wait()


def finish(*refs):
    ins, outs, held, sem = refs[:8], refs[8:18], refs[18:28], refs[28]
    parts = [(k, r) for r in range(ROWS) for k in range(2)] + [(k, None) for k in range(2, 10)]

    def move(way, n):
        k, r = parts[n]
        src, dst = ((ins, held), (held, outs))[way]
        if r is None:
            return pltpu.make_async_copy(src[k], dst[k], sem.at[way, n])
        return pltpu.make_async_copy(src[k].at[r], dst[k].at[r], sem.at[way, n])

    incoming = [move(0, n) for n in range(13)]
    for copy in incoming:
        copy.start()
    small = ins[7]
    held[7][...] = small[1]
    held[8][...] = small[0]
    held[9][...] = small[2:5, 0:CH]
    outgoing = [move(1, n) for n in range(13, 16)]
    for copy in outgoing:
        copy.start()
    for n, copy in enumerate(incoming):
        copy.wait()
        outgoing.append(move(1, n))
        outgoing[-1].start()
    for copy in outgoing:
        copy.wait()


def on_device(
    tokens, start_flags, norm_one, w_in, w_conv, w_out, norm_two, w_gate, w_up, w_down, cotangent
):
    any_spec = pl.BlockSpec(memory_space=pl.ANY)
    vmem = pl.BlockSpec(memory_space=pltpu.VMEM)
    dma = pltpu.SemaphoreType.DMA
    shape = jax.ShapeDtypeStruct
    outs = pl.pallas_call(
        kernel,
        out_shape=(
            shape((ROWS, TB, D), F32),
            shape((ROWS, TB, D), F32),
            shape((3, 32, CH), F32),
            shape((32, CH), F32),
            shape((32, HID), F32),
            shape((32, HID), F32),
            shape((32, HID), F32),
            shape((8, D), F32),
        ),
        in_specs=[pl.BlockSpec(memory_space=pltpu.SMEM)] + [any_spec] * 7 + [vmem] * 3,
        out_specs=(any_spec,) * 8,
        scratch_shapes=[
            pltpu.VMEM((ROWS, TB, D), F32),
            pltpu.VMEM((ROWS, TB, D), F32),
            pltpu.VMEM((3, D, CH), BF16),
            pltpu.VMEM((D, CH), BF16),
            pltpu.VMEM((D, HID), BF16),
            pltpu.VMEM((D, HID), BF16),
            pltpu.VMEM((D, HID), BF16),
            pltpu.VMEM((3, POS, CH), F32),
            pltpu.VMEM((ROWS, TB + 8, CH), F32),
            pltpu.VMEM((ROWS, TB + 8, CH), F32),
            pltpu.VMEM((ROWS, TB, D), F32),
            pltpu.VMEM((POS, D), BF16),
            pltpu.VMEM((POS, HID), BF16),
            pltpu.VMEM((POS, HID), BF16),
            pltpu.VMEM((POS, HID), BF16),
            pltpu.VMEM((2, POS, POS), BF16),
            pltpu.VMEM((POS, HID), F32),
                pltpu.VMEM((ROWS, 8, CH), F32),
            pltpu.VMEM((ROWS, 8, CH), F32),
            pltpu.VMEM((ROWS, 8, CH), F32),
            pltpu.VMEM((2, ROWS, TB, D), F32),
            pltpu.VMEM((2, ROWS, HALF, D), F32),
            pltpu.VMEM((3, ROWS, HALF, D), F32),
            pltpu.VMEM((2, ROWS, HALF, D), F32),
            pltpu.VMEM((2, 4, 4, 2, 32, HID), F32),
            pltpu.VMEM((2, 2, 2, 2, 32, HID), F32),
            pltpu.VMEM((2, 2, 2, 4, 32, HID), F32),
            pltpu.VMEM((4, 2, 2, 16, HID), F32),
            pltpu.VMEM((4, 2, 2, 32, HID), F32),
            pltpu.VMEM((4, 32, HID), F32),
            pltpu.VMEM((4, 4, 2, 32, CH), F32),
            pltpu.VMEM((4, 4, 32, CH), F32),
            pltpu.VMEM((8, D), F32),
            pltpu.VMEM((3, 4, 8, D), F32),
            dma((7,)),
            dma((16,)),
            dma((3, 3)),
            dma((3, 3)),
            dma((22,)),
            dma((22,)),
            dma((3,)),
            dma((3,)),
            dma((2, 2)),
            dma((3, 2)),
            dma((2, 2)),
            dma((3, 2)),
            dma((2, 2)),
            dma((3, 2)),
            dma((3, 2, 6)),
            dma((3, 2, 6)),
            dma((2, 4)),
            dma((2, 4)),
            dma((3, 2, 6)),
            dma((5, 2, 6)),
            dma((4,)),
            dma((4,)),
            dma((1,)),
            dma((1,)),
            dma((3,)),
            dma((3, 4)),
            pltpu.SemaphoreType.REGULAR((2, 2, 2)),
        ],
        compiler_params=pltpu.CompilerParams(
            collective_id=0, has_side_effects=True, vmem_limit_bytes=63 * 2**20
        ),
        name="block",
    )(
        start_flags.T, tokens, cotangent, w_in, w_out, w_gate, w_up, w_down,
        norm_one.reshape(1, D), norm_two.reshape(1, D), w_conv,
    )
    result, grad_tokens, g_in, g_out, g_gate, g_up, g_down, one, two, taps = pl.pallas_call(
        finish,
        out_shape=tuple(shape(o.shape, F32) for o in outs[:2])
        + (
            shape((3, 32, CH), F32),
            shape((32, CH), F32),
            shape((32, HID), F32),
            shape((32, HID), F32),
            shape((32, HID), F32),
            shape((D,), F32),
            shape((D,), F32),
            shape((3, CH), F32),
        ),
        in_specs=[any_spec] * 7 + [vmem],
        out_specs=(any_spec,) * 10,
        scratch_shapes=[pltpu.VMEM(o.shape, F32) for o in outs[:7]]
        + [pltpu.VMEM(d, F32) for d in ((D,), (D,), (3, CH))]
        + [dma((2, 16))],
        compiler_params=pltpu.CompilerParams(vmem_limit_bytes=60 * 2**20),
        name="finish",
    )(*outs)
    return result, grad_tokens, one, g_in, taps, g_out, two, g_gate, g_up, g_down


def solution(mesh):
    return jax.shard_map(
        on_device,
        mesh=mesh,
        in_specs=(
            P(None, "seq", None),
            P(None, "seq"),
            P(),
            P(None, None, "wt"),
            P(None, "wt"),
            P(None, "wt"),
            P(),
            P(None, "wt"),
            P(None, "wt"),
            P(None, "wt"),
            P(None, "seq", None),
        ),
        out_specs=(
            P(None, "seq", None),
            P(None, "seq", None),
            P(),
            P(None, "seq", "wt"),
            P(None, "wt"),
            P("seq", "wt"),
            P(),
            P("seq", "wt"),
            P("seq", "wt"),
            P("seq", "wt"),
        ),
        check_vma=False,
    )
```
